32 devices in a mesh: prompt: 8 (over y, x, core), sample: 4 (over z).
Axes of the slice: x: 2, y: 2, z: 4, core: 2. Of those that a mesh axis runs over, the one named last changes fastest.
Arguments:
- queries: bfloat16 [8, 2048, 1792], P('prompt', 'sample'), may hold values from -60 to 60
- prompt_keys: bfloat16 [8, 1024, 256], P('prompt', 'sample'), may hold values from -4 to 4
- prompt_value_rows: bfloat16 [8, 1024, 256], P('prompt', 'sample'), may hold values from -4 to 4
- reply_keys: bfloat16 [8, 2048, 256], P('prompt', 'sample'), may hold values from -4 to 4
- response_values: bfloat16 [8, 2048, 256], P('prompt', 'sample'), may hold values from -4 to 4
- lengths: int32 [8, 4], P('prompt'), may hold values from 1 to 4, as said below
- hand_counts: int32 [8, 4, 2], P('prompt'), may hold values from 0 to 2, as said below
Outputs:
- attended: bfloat16 [8, 2048, 1792], P('prompt', 'sample')
The draws below stay inside these ranges and needn't reach their ends.
Inputs may be any that keep to these rules, and one draw needn't show every extreme that they name: lengths[p, s] counts the live tiles of response s; some response of every prompt has 4 tiles. hand_counts[p, s, k] is the number of tiles that device s hands to its section-k partner; of two partners at most one hands tiles, and every load stays between 1 and 4.
All inputs are finite; a program needn't handle non-finite values.
Results may differ from the reference program's by a relative error of at most 0.0038.
Values may be sent and summed in bfloat16 or wider, within the bound.
No kernel may reach another device: no remote copies, remote signals or barrier semaphores. Data moves between devices by JAX's collectives and lax.ppermute only.
A program may use at most 64 MiB of HBM per device.

```python
import math
import jax
import jax.numpy as jnp
from jax import lax

HQ = 14
KEY_VALUE_HEADS = 2
QUERY_PER_KEY = 7
HEAD_WIDTH = 128
TILE_TOKENS = 128
MOST_TILES = 4
SECTIONS = 2
PROMPT_LENGTH = 1024
PROMPT_COUNT = 8
RESPONSE_ROWS = 2048
N_SAMPLE = 4


def random_source(key, dims, spread, limit):
    return jnp.clip(jax.random.normal(key, dims, jnp.float32) * spread, -limit, limit)


def key_fields(key):
    prefix_tokens = random_source(jax.random.fold_in(key, 11), (PROMPT_COUNT, PROMPT_LENGTH, KEY_VALUE_HEADS * HEAD_WIDTH), 1.0, 4.0)
    answer_output = random_source(jax.random.fold_in(key, 12), (PROMPT_COUNT, N_SAMPLE * MOST_TILES * TILE_TOKENS, KEY_VALUE_HEADS * HEAD_WIDTH), 1.0, 4.0)
    return (prefix_tokens, answer_output)


def draw_queries(key, part):
    base_field = random_source(jax.random.fold_in(key, 13), (PROMPT_COUNT, N_SAMPLE * MOST_TILES * TILE_TOKENS, HQ * HEAD_WIDTH), 2.0, 12.0)
    return base_field.astype(jnp.bfloat16)


def draw_prompt_keys(key, part):
    return key_fields(key)[0].astype(jnp.bfloat16)


def draw_reply_keys(key, part):
    return key_fields(key)[1].astype(jnp.bfloat16)


def balance_plan(key):
    source_key = jax.random.fold_in(key, 7)
    first_draw = jax.random.randint(jax.random.fold_in(source_key, 1), (PROMPT_COUNT, N_SAMPLE), 1, MOST_TILES + 1)
    second_draw = jax.random.randint(jax.random.fold_in(source_key, 2), (PROMPT_COUNT, N_SAMPLE), 1, MOST_TILES + 1)
    length_table = jnp.minimum(first_draw, second_draw).astype(jnp.int32)
    length_table = length_table.at[:, 0].set(MOST_TILES).at[:, N_SAMPLE // 2].set(1)
    coins = jax.random.randint(jax.random.fold_in(source_key, 3), (PROMPT_COUNT, SECTIONS, N_SAMPLE), 0, 2).astype(jnp.int32)
    coins = coins.at[:, 0, 0].set(1)
    devices = jnp.arange(N_SAMPLE, dtype=jnp.int32)
    top_bit = N_SAMPLE.bit_length() - 1
    burden = length_table
    handed = []
    for section_index in range(SECTIONS):
        partner = devices ^ 1 << top_bit - 1 - section_index
        lower = jnp.minimum(devices, partner)
        rounding = coins[:, section_index][:, lower]
        spread_now = burden - burden[:, partner]
        giving = jnp.where(spread_now > 0, (spread_now + rounding) // 2, 0).astype(jnp.int32)
        handed.append(giving)
        burden = burden - giving + giving[:, partner]
    return (length_table, jnp.stack(handed, axis=-1))


def draw_lengths(key, part):
    return balance_plan(key)[0]


def draw_hand_counts(key, part):
    return balance_plan(key)[1]


def block_scale(own_key, extent, cuts, least, largest):
    def one(axis_at, shards_of):
        heights = jax.random.uniform(jax.random.fold_in(jax.random.fold_in(own_key, 6), axis_at), (shards_of,), jnp.float32, least / len(cuts), largest / len(cuts))
        return jnp.repeat(jnp.exp(heights), extent[axis_at] // shards_of).reshape((-1,) + (1,) * (len(extent) - axis_at - 1))

    loudness = one(*cuts[0])
    for cut in cuts[1:]:
        loudness = loudness * one(*cut)
    return loudness


def noise(rng, extent, width, most, split=(), kind=jnp.bfloat16):
    entries = jax.random.normal(rng, extent, jnp.float32) * width
    if len(split) > 0:
        entries = block_scale(rng, extent, split, -0.22, 0.18) * entries
    return jnp.clip(entries, min=-most, max=most).astype(kind)


def setup_inputs(seed: int = 0) -> dict:
    streams_of = jax.random.split(jax.random.key(seed), 8)
    queries = draw_queries(jax.random.fold_in(streams_of[7], 71), 0)
    prompt_keys = draw_prompt_keys(jax.random.fold_in(streams_of[7], 71), 0)
    prompt_value_rows = noise(streams_of[2], (PROMPT_COUNT, PROMPT_LENGTH, KEY_VALUE_HEADS * HEAD_WIDTH), 1.0, 4.0, ((0, 8), (1, 4)))
    reply_keys = draw_reply_keys(jax.random.fold_in(streams_of[7], 71), 0)
    response_values = noise(streams_of[4], (PROMPT_COUNT, RESPONSE_ROWS, KEY_VALUE_HEADS * HEAD_WIDTH), 1.0, 4.0, ((0, 8), (1, 4)))
    lengths = draw_lengths(jax.random.fold_in(streams_of[7], 71), 0)
    hand_counts = draw_hand_counts(jax.random.fold_in(streams_of[7], 71), 0)
    return {"queries": queries, "prompt_keys": prompt_keys, "prompt_value_rows": prompt_value_rows, "reply_keys": reply_keys, "response_values": response_values, "lengths": lengths, "hand_counts": hand_counts}


def attend(query_tile_rows, key_row_block, value_row_block, allowed):
    query_head_block = query_tile_rows.astype(jnp.float32).reshape(TILE_TOKENS, KEY_VALUE_HEADS, QUERY_PER_KEY, HEAD_WIDTH)
    key_head_block = key_row_block.astype(jnp.float32).reshape(-1, KEY_VALUE_HEADS, HEAD_WIDTH)
    value_head_block = value_row_block.astype(jnp.float32).reshape(-1, KEY_VALUE_HEADS, HEAD_WIDTH)
    scores = jnp.einsum('tkgd,skd->kgts', query_head_block, key_head_block) * (1.0 / math.sqrt(HEAD_WIDTH))
    if allowed is not None:
        scores = jnp.where(allowed, scores, -1e+30)
    maxima = lax.optimization_barrier(jnp.max(scores, axis=-1, keepdims=True))
    exponent = jnp.exp(scores - maxima)
    totals = lax.optimization_barrier(jnp.sum(exponent, axis=-1, keepdims=True))
    weights = lax.optimization_barrier(exponent.astype(jnp.bfloat16)).astype(jnp.float32)
    blended_output = jnp.einsum('kgts,skd->tkgd', weights, value_head_block) / jnp.transpose(totals, (2, 0, 1, 3))
    levels = maxima[..., 0] + jnp.log(totals[..., 0])
    return (blended_output, levels)

def combine(first_mix, first_level, second_mix, second_level):
    ceiling = jnp.maximum(first_level, second_level)
    first_weight = jnp.transpose(jnp.exp(first_level - ceiling), (2, 0, 1))[..., None]
    second_weight = jnp.transpose(jnp.exp(second_level - ceiling), (2, 0, 1))[..., None]
    blended_output = (first_weight * first_mix + second_weight * second_mix) / (first_weight + second_weight)
    return blended_output.reshape(TILE_TOKENS, KEY_VALUE_HEADS * QUERY_PER_KEY * HEAD_WIDTH).astype(jnp.bfloat16)

def settle(length_row, hand_rows):
    devices = jnp.arange(N_SAMPLE, dtype=jnp.int32)
    slot_ids = jnp.arange(MOST_TILES, dtype=jnp.int32)
    slot_table = jnp.where(slot_ids[None, :] < length_row[:, None], devices[:, None] * MOST_TILES + slot_ids[None, :], -1)
    burden = length_row
    top_bit = N_SAMPLE.bit_length() - 1
    for section_index in range(SECTIONS):
        partner = devices ^ 1 << top_bit - 1 - section_index
        giving = hand_rows[:, section_index]
        getting = giving[partner]
        keeping = burden - giving
        offset = slot_ids[None, :] - keeping[:, None]
        source = jnp.clip(burden[partner][:, None] - getting[:, None] + offset, 0, MOST_TILES - 1)
        incoming = jnp.take_along_axis(slot_table[partner], source, axis=1)
        slot_table = jnp.where(offset < 0, slot_table, jnp.where(offset < getting[:, None], incoming, -1))
        burden = keeping + getting
    return slot_table

def reference(queries, prompt_keys, prompt_value_rows, reply_keys, response_values, lengths, hand_counts):

    def one_prompt(pieces):
        query_rows, key_prompt, value_prompt, key_reply, value_reply, length_row, hand_rows = pieces
        query_tiles = query_rows.reshape(N_SAMPLE * MOST_TILES, TILE_TOKENS, -1)
        offsets = jnp.arange(TILE_TOKENS, dtype=jnp.int32)
        positions = jnp.arange(MOST_TILES * TILE_TOKENS, dtype=jnp.int32)

        def one_tile(number):
            sample = number // MOST_TILES
            within = number % MOST_TILES
            query_tile_rows = query_tiles[number]
            first_row = (sample * MOST_TILES * TILE_TOKENS).astype(jnp.int32)
            own_keys = lax.dynamic_slice_in_dim(key_reply, first_row, MOST_TILES * TILE_TOKENS, 0)
            own_values = lax.dynamic_slice_in_dim(value_reply, first_row, MOST_TILES * TILE_TOKENS, 0)
            allowed = positions[None, :] <= (within * TILE_TOKENS + offsets)[:, None]
            reply_mix, reply_level = attend(query_tile_rows, own_keys, own_values, allowed)
            reply_mix = lax.optimization_barrier(reply_mix.astype(jnp.bfloat16)).astype(jnp.float32)
            prompt_mix, prompt_level = attend(query_tile_rows, key_prompt, value_prompt, None)
            result = combine(prompt_mix, prompt_level, reply_mix, reply_level)
            is_live = within < length_row[sample]
            return jnp.where(is_live, result, jnp.zeros_like(result))
        results = lax.map(one_tile, jnp.arange(N_SAMPLE * MOST_TILES, dtype=jnp.int32))
        slot_table = settle(length_row, hand_rows)
        placed = results[jnp.clip(slot_table, 0, N_SAMPLE * MOST_TILES - 1)]
        placed = jnp.where((slot_table >= 0)[:, :, None, None], placed, jnp.zeros_like(placed))
        return placed.reshape(N_SAMPLE * MOST_TILES * TILE_TOKENS, -1)
    return lax.map(one_prompt, (queries, prompt_keys, prompt_value_rows, reply_keys, response_values, lengths, hand_counts))
```

```python
import functools
import math

import jax
import jax.numpy as jnp
from jax import lax
from jax.experimental import pallas as pl
from jax.experimental.pallas import tpu as pltpu
from jax.sharding import PartitionSpec as P

KEY_VALUE_HEADS = 2
QUERY_PER_KEY = 7
HEAD_WIDTH = 128
TILE_TOKENS = 128
MOST_TILES = 4
SECTIONS = 2
HEADS = KEY_VALUE_HEADS * QUERY_PER_KEY
COLUMNS = HEADS * HEAD_WIDTH
KEY_COLUMNS = KEY_VALUE_HEADS * HEAD_WIDTH
SCALE = math.log2(math.e) / math.sqrt(HEAD_WIDTH)
MASKED = -1e30
TRANSPOSED = (((1,), (1,)), ((), ()))


def head_columns(group, head):
    first = (group * QUERY_PER_KEY + head) * HEAD_WIDTH
    return slice(first, first + HEAD_WIDTH)


def attend_body(pieces, with_reply, with_state, last, length_ref, query_ref, *refs):
    refs = list(refs)
    blocks = [(refs.pop(0), refs.pop(0)) for _ in range(pieces + with_reply)]
    state = (refs.pop(0), refs.pop(0)) if with_state else None
    tile = pl.program_id(0)
    live = tile < length_ref[0]

    @pl.when(live)
    def _():
        lanes = lax.broadcasted_iota(jnp.int32, (TILE_TOKENS, HEAD_WIDTH), 1)
        levels = jnp.zeros((TILE_TOKENS, HEAD_WIDTH), jnp.float32)
        for group in range(KEY_VALUE_HEADS):
            columns = slice(group * HEAD_WIDTH, (group + 1) * HEAD_WIDTH)
            rows = jnp.concatenate(
                [query_ref[:, head_columns(group, head)] for head in range(QUERY_PER_KEY)], axis=0
            )
            scores = []
            for number, (key_ref, _) in enumerate(blocks):
                block = lax.dot_general(
                    rows, key_ref[:, columns], TRANSPOSED, preferred_element_type=jnp.float32
                )
                if with_reply and number == pieces:
                    row = lax.broadcasted_iota(jnp.int32, block.shape, 0) % TILE_TOKENS
                    column = lax.broadcasted_iota(jnp.int32, block.shape, 1)
                    block = jnp.where(column - row <= tile * TILE_TOKENS, block, MASKED)
                scores.append(block)
            top = functools.reduce(
                jnp.maximum, [jnp.max(block, axis=1, keepdims=True) for block in scores]
            )
            total = 0.0
            mix = 0.0
            for block, (_, value_ref) in zip(scores, blocks):
                weights = jnp.exp2((block - top) * SCALE)
                total = total + jnp.sum(weights, axis=1, keepdims=True)
                mix = mix + jnp.dot(
                    weights.astype(jnp.bfloat16),
                    value_ref[:, columns],
                    preferred_element_type=jnp.float32,
                )
            top = top * SCALE
            for head in range(QUERY_PER_KEY):
                part = slice(head * TILE_TOKENS, (head + 1) * TILE_TOKENS)
                where = head_columns(group, head)
                index = group * QUERY_PER_KEY + head
                head_top, head_total, head_mix = top[part], total[part], mix[part]
                if with_state:
                    before = state[1][:, index : index + 1]
                    ceiling = jnp.maximum(before, head_top)
                    old, new = jnp.exp2(before - ceiling), jnp.exp2(head_top - ceiling)
                    head_mix = old * state[0][:, where] + new * head_mix
                    head_total = old + new * head_total
                    head_top = ceiling
                mixed = head_mix * (1.0 / head_total)
                if last:
                    refs[0][:, where] = mixed.astype(jnp.bfloat16)
                else:
                    refs[0][:, where] = mixed
                    level = head_top + jnp.log2(head_total)
                    levels = jnp.where(lanes == index, level, levels)
        if not last:
            refs[1][...] = levels

    if last:
        @pl.when(jnp.logical_not(live))
        def _():
            refs[0][...] = jnp.zeros((TILE_TOKENS, COLUMNS), jnp.bfloat16)


def attend(length, queries, pieces, reply=None, state=None, last=False):
    blocks = pieces + ([reply] if reply is not None else [])
    tile_of = lambda tile, length: (tile, 0)
    whole = lambda tile, length: (0, 0)
    wide = pl.BlockSpec((TILE_TOKENS, COLUMNS), tile_of)
    narrow = pl.BlockSpec((TILE_TOKENS, HEAD_WIDTH), tile_of)
    in_specs, operands = [wide], [queries]
    keys = 0
    for block in blocks:
        keys += block[0].shape[0]
        in_specs += [pl.BlockSpec(array.shape, whole) for array in block]
        operands += list(block)
    if state is not None:
        in_specs += [wide, narrow]
        operands += list(state)
    rows = queries.shape[0]
    if last:
        out_specs = wide
        out_shape = jax.ShapeDtypeStruct((rows, COLUMNS), jnp.bfloat16)
    else:
        out_specs = (wide, narrow)
        out_shape = (
            jax.ShapeDtypeStruct((rows, COLUMNS), jnp.float32),
            jax.ShapeDtypeStruct((rows, HEAD_WIDTH), jnp.float32),
        )
    body = functools.partial(
        attend_body, len(pieces), reply is not None, state is not None, last
    )
    return pl.pallas_call(
        body,
        grid_spec=pltpu.PrefetchScalarGridSpec(
            num_scalar_prefetch=1,
            grid=(rows // TILE_TOKENS,),
            in_specs=in_specs,
            out_specs=out_specs,
        ),
        out_shape=out_shape,
        cost_estimate=pl.CostEstimate(
            flops=4 * rows * keys * COLUMNS,
            bytes_accessed=8 * rows * COLUMNS,
            transcendentals=rows * keys * HEADS,
        ),
        compiler_params=pltpu.CompilerParams(vmem_limit_bytes=48 << 20),
    )(length, *operands)


def swap(value, distance):
    members = lax.axis_size("sample")
    return lax.ppermute(value, "sample", [(source, source ^ distance) for source in range(members)])


def per_device(
    queries, prompt_keys, prompt_value_rows, reply_keys, response_values, lengths, hand_counts
):
    members = lax.axis_size("sample")
    top_bit = members.bit_length() - 1
    my_index = lax.axis_index("sample")
    own = (prompt_keys[0], prompt_value_rows[0])

    held = [own]
    for bit in reversed(range(top_bit)):
        arrived = [tuple(swap(array, 2**bit) for array in block) for block in held]
        held += arrived
    near, far = held[:1], held[1:]

    length = lax.dynamic_slice_in_dim(lengths[0], my_index, 1)
    state = attend(length, queries[0], near, reply=(reply_keys[0], response_values[0]))
    outputs = attend(length, queries[0], far, state=state, last=True)

    load = length[0]
    for section in range(SECTIONS):
        distance = 2 ** (top_bit - 1 - section)
        hands = hand_counts[0, :, section]
        giving = lax.dynamic_index_in_dim(hands, my_index, keepdims=False)
        getting = lax.dynamic_index_in_dim(hands, my_index ^ distance, keepdims=False)
        keeping = load - giving

        def trade(count, outputs, keeping, distance=distance):
            if count == 0:
                return outputs
            top_rows = lax.dynamic_slice_in_dim(
                outputs, keeping * TILE_TOKENS, count * TILE_TOKENS, 0
            )
            return lax.dynamic_update_slice_in_dim(
                outputs, swap(top_rows, distance), keeping * TILE_TOKENS, 0
            )

        outputs = lax.switch(
            jnp.maximum(giving, getting),
            [functools.partial(trade, count) for count in range(3)],
            outputs,
            keeping,
        )
        load = keeping + getting
    return outputs[None]


def solution(mesh):
    placed = (
        P("prompt", "sample", None),
        P("prompt", "sample", None),
        P("prompt", "sample", None),
        P("prompt", "sample", None),
        P("prompt", "sample", None),
        P("prompt", None),
        P("prompt", None, None),
    )
    return jax.shard_map(
        per_device,
        mesh=mesh,
        in_specs=placed,
        out_specs=P("prompt", "sample", None),
        check_vma=False,
    )
```

```python
import functools
import math

import jax
import jax.numpy as jnp
from jax import lax
from jax.experimental import pallas as pl
from jax.experimental.pallas import tpu as pltpu
from jax.sharding import PartitionSpec as P

KEY_VALUE_HEADS = 2
QUERY_PER_KEY = 7
HEAD_WIDTH = 128
TILE_TOKENS = 128
MOST_TILES = 4
SECTIONS = 2
HAND = 2
GROUP_COLUMNS = QUERY_PER_KEY * HEAD_WIDTH
COLUMNS = KEY_VALUE_HEADS * GROUP_COLUMNS
SCALE = math.log2(math.e) / math.sqrt(HEAD_WIDTH)
MASKED = -1e30
TRANSPOSED = (((1,), (1,)), ((), ()))
JOBS = ((0, 4), (4, 7))

BUNDLES = (
    (((0, 2),), ((0, 3),)),
    (((0, 2),), ((0, 2),)),
    (((0, 2), (3, 1)), ((0, 3),)),
    (((0, 2),), ((0, 3),), ((0, 1),)),
    (((0, 2), (1, 3)), ((0, 2),)),
    (((0, 2), (3, 1)), ((0, 2),)),
    (((0, 2), (1, 3)), ((0, 3),)),
    (((0, 2), (2, 0), (1, 3), (3, 1)), ((0, 2), (2, 0), (1, 3), (3, 1)),
     ((0, 3), (3, 0), (1, 2), (2, 1)), ((0, 1), (1, 0), (2, 3), (3, 2))),
)
SEND, FILL, KEPT, PLAN = 0, 6, 12, 16


def entry(distance, turn):
    return (distance - 1) * HAND + turn


def bundle_entries(bundle):
    entries, capacity = [], {}
    for permute in bundle:
        (distance,) = {source ^ target for source, target in permute}
        turn = sum(1 for other, _ in entries if other == distance)
        entries.append((distance, turn))
        for source, _ in permute:
            assert capacity.get((source, distance), 0) == turn
            capacity[source, distance] = turn + 1
    return [entry(*at) for at in entries], capacity


def plan_body(members, lengths_ref, hands_ref, plan_ref, choice_ref):
    me = lax.axis_index("sample")
    far, near = members // 2, members // 4

    def counts(device):
        partner = device ^ far
        first = hands_ref[0, device, 0]
        through = jnp.minimum(hands_ref[0, partner, 1], first)
        second = jnp.maximum(hands_ref[0, device, 1] - hands_ref[0, partner, 0], 0)
        return {1: second, 2: first - through, 3: through}

    mine = counts(me)
    kept = lengths_ref[0, me] - mine[1] - mine[2] - mine[3]
    arriving = {2: counts(me ^ far)[2], 1: counts(me ^ near)[1], 3: counts(me ^ far ^ near)[3]}
    tile = slot = kept
    for distance in (1, 2, 3):
        for turn in range(HAND):
            plan_ref[SEND + entry(distance, turn)] = jnp.where(
                turn < mine[distance], tile + turn, -1
            )
        tile = tile + mine[distance]
    for distance in (2, 1, 3):
        for turn in range(HAND):
            plan_ref[FILL + entry(distance, turn)] = jnp.where(
                turn < arriving[distance], slot + turn, -1
            )
        slot = slot + arriving[distance]
    for index in range(KEPT, PLAN):
        plan_ref[index] = kept

    needs = {}
    for device in range(members):
        for distance, count in counts(device).items():
            key = (device // near, distance)
            needs[key] = jnp.maximum(needs[key], count) if key in needs else count
    choice = jnp.int32(len(BUNDLES))
    for number in reversed(range(len(BUNDLES))):
        _, capacity = bundle_entries(BUNDLES[number])
        lacking = jnp.int32(0)
        for key, count in needs.items():
            lacking = lacking + jnp.maximum(count - capacity.get(key, 0), 0)
        choice = jnp.where(lacking == 0, number, choice)
    choice_ref[0] = choice


def make_plan(members, lengths, hand_counts):
    in_smem = pl.BlockSpec(memory_space=pltpu.SMEM)
    return pl.pallas_call(
        functools.partial(plan_body, members),
        in_specs=[in_smem, in_smem],
        out_specs=(in_smem, in_smem),
        out_shape=(
            jax.ShapeDtypeStruct((PLAN,), jnp.int32),
            jax.ShapeDtypeStruct((1,), jnp.int32),
        ),
    )(lengths, hand_counts)


def attend_tile(tile, query_ref, block_refs, reply_key_ref, reply_value_ref, store):
    def score(job):
        first, last = job
        rows = jnp.concatenate(
            [query_ref[:, head * HEAD_WIDTH : (head + 1) * HEAD_WIDTH] for head in range(first, last)],
            axis=0,
        )
        scores = [
            lax.dot_general(
                rows, block[:, :HEAD_WIDTH], TRANSPOSED, preferred_element_type=jnp.float32
            )
            for block in block_refs
        ]
        reply = lax.dot_general(
            rows, reply_key_ref[...], TRANSPOSED, preferred_element_type=jnp.float32
        )
        row = lax.broadcasted_iota(jnp.int32, reply.shape, 0) % TILE_TOKENS
        column = lax.broadcasted_iota(jnp.int32, reply.shape, 1)
        scores.append(jnp.where(column - row <= tile * TILE_TOKENS, reply, MASKED))
        return scores

    def finish(job, scores):
        first, last = job
        top = functools.reduce(
            jnp.maximum, [jnp.max(block, axis=1, keepdims=True) for block in scores]
        )
        values = [block[:, HEAD_WIDTH:] for block in block_refs] + [reply_value_ref[...]]
        total = mix = 0.0
        for block, value in zip(scores, values):
            weights = jnp.exp2((block - top) * SCALE)
            total = total + jnp.sum(weights, axis=1, keepdims=True)
            mix = mix + jnp.dot(
                weights.astype(jnp.bfloat16), value, preferred_element_type=jnp.float32
            )
        mix = (mix * (1.0 / total)).astype(jnp.bfloat16)
        for head in range(first, last):
            part = (head - first) * TILE_TOKENS
            store(
                slice(head * HEAD_WIDTH, (head + 1) * HEAD_WIDTH), mix[part : part + TILE_TOKENS]
            )

    ahead = score(JOBS[0])
    for number, job in enumerate(JOBS):
        scores = ahead
        if number + 1 < len(JOBS):
            ahead = score(JOBS[number + 1])
        finish(job, scores)


def chosen(table, step):
    value = jnp.int32(table[0])
    for number in range(1, len(table)):
        value = jnp.where(step == number, table[number], value)
    return value


def leaving_body(entries, blocks, plan_ref, query_ref, *refs):
    step = pl.program_id(0)
    tile = plan_ref[SEND + chosen(entries, step)]
    outputs = refs[blocks + 2 :]

    @pl.when(tile >= 0)
    def _():
        def store(columns, value):
            for number, output in enumerate(outputs):
                @pl.when(step == number)
                def _():
                    output[:, columns] = value

        attend_tile(tile, query_ref, refs[:blocks], refs[blocks], refs[blocks + 1], store)


def kept_body(blocks, plan_ref, query_ref, *refs):
    tile = pl.program_id(0)
    output = refs[-1]

    @pl.when(tile < plan_ref[KEPT])
    def _():
        def store(columns, value):
            output[:, columns] = value

        attend_tile(tile, query_ref, refs[:blocks], refs[blocks], refs[blocks + 1], store)

    @pl.when(tile >= plan_ref[KEPT])
    def _():
        output[...] = jnp.zeros(output.shape, output.dtype)


def attend(plan, queries, group, blocks, reply, entries=None, into=None):
    rows = queries.shape[0]
    tile_shape = (TILE_TOKENS, GROUP_COLUMNS)
    whole = lambda step, plan: (0, 0)
    if entries is not None:
        steps = len(entries)
        body = functools.partial(leaving_body, entries, len(blocks))
        query_at = lambda step, plan: (jnp.maximum(plan[SEND + chosen(entries, step)], 0), group)
        out_specs = [pl.BlockSpec(tile_shape, whole) for _ in entries]
        out_shape = [jax.ShapeDtypeStruct(tile_shape, jnp.bfloat16) for _ in entries]
    else:
        steps = rows // TILE_TOKENS
        body = functools.partial(kept_body, len(blocks))
        query_at = lambda step, plan: (step, group)
        out_specs = pl.BlockSpec(tile_shape, query_at)
        out_shape = jax.ShapeDtypeStruct((rows, COLUMNS), jnp.bfloat16)
    reply_spec = pl.BlockSpec(
        (reply[0].shape[0], HEAD_WIDTH), lambda step, plan: (0, group)
    )
    in_specs = [pl.BlockSpec(tile_shape, query_at)]
    in_specs += [pl.BlockSpec(block.shape, whole) for block in blocks]
    in_specs += [reply_spec, reply_spec]
    operands = [plan, queries, *blocks, *reply]
    aliases = {}
    if into is not None:
        aliases = {len(operands): 0}
        in_specs.append(pl.BlockSpec(memory_space=pl.ANY))
        operands.append(into)
    keys = sum(block.shape[0] for block in blocks) + reply[0].shape[0]
    return pl.pallas_call(
        body,
        grid_spec=pltpu.PrefetchScalarGridSpec(
            num_scalar_prefetch=1, grid=(steps,), in_specs=in_specs, out_specs=out_specs
        ),
        out_shape=out_shape,
        input_output_aliases=aliases,
        cost_estimate=pl.CostEstimate(
            flops=4 * 2 * TILE_TOKENS * keys * GROUP_COLUMNS,
            bytes_accessed=8 * TILE_TOKENS * GROUP_COLUMNS,
            transcendentals=2 * TILE_TOKENS * keys * QUERY_PER_KEY,
        ),
        compiler_params=pltpu.CompilerParams(vmem_limit_bytes=40 << 20),
    )(*operands)


def assemble_body(places, plan_ref, *refs):
    arrived, output, semaphores = refs[: len(places)], refs[-2], refs[-1]
    copies = []
    for number, (where, group) in enumerate(places):
        slot = plan_ref[FILL + where]
        first = pl.multiple_of(jnp.maximum(slot, 0) * TILE_TOKENS, TILE_TOKENS)
        copy = pltpu.make_async_copy(
            arrived[number],
            output.at[
                pl.ds(first, TILE_TOKENS), pl.ds(group * GROUP_COLUMNS, GROUP_COLUMNS)
            ],
            semaphores.at[number],
        )
        copies.append((slot >= 0, copy))
    for taken, copy in copies:
        pl.when(taken)(copy.start)
    for taken, copy in copies:
        pl.when(taken)(copy.wait)


def assemble(plan, arrived, places, output):
    anywhere = pl.BlockSpec(memory_space=pl.ANY)
    return pl.pallas_call(
        functools.partial(assemble_body, places),
        in_specs=[pl.BlockSpec(memory_space=pltpu.SMEM)] + [anywhere] * (len(places) + 1),
        out_specs=anywhere,
        out_shape=jax.ShapeDtypeStruct(output.shape, output.dtype),
        scratch_shapes=[pltpu.SemaphoreType.DMA((len(places),))],
        input_output_aliases={len(places) + 1: 0},
    )(plan, *arrived, output)


def swap(value, distance):
    members = lax.axis_size("sample")
    return lax.ppermute(value, "sample", [(source, source ^ distance) for source in range(members)])


def gather(own):
    held = [own]
    distance = lax.axis_size("sample") // 2
    while distance:
        held += [swap(block, distance) for block in held]
        distance //= 2
    return held


def run_bundle(bundle, plan, queries, packed, reply, lengths, hand_counts):
    quarter = lax.axis_size("sample") // 4
    entries, _ = bundle_entries(bundle)
    held = [gather(block) for block in packed]
    arrived, places = [], []
    for group in range(KEY_VALUE_HEADS):
        leaving = attend(plan, queries, group, held[group], reply, entries=entries)
        for permute, where, tile in zip(bundle, entries, leaving):
            pairs = [
                (source * quarter + low, target * quarter + low)
                for source, target in permute
                for low in range(quarter)
            ]
            arrived.append(lax.ppermute(tile, "sample", pairs))
            places.append((where, group))
    output = None
    for group in range(KEY_VALUE_HEADS):
        output = attend(plan, queries, group, held[group], reply, into=output)
    return assemble(plan, arrived, places, output)


def run_chain(plan, queries, packed, reply, lengths, hand_counts):
    members = lax.axis_size("sample")
    my_index = lax.axis_index("sample")
    load = lax.dynamic_index_in_dim(lengths[0], my_index, keepdims=False)
    everything = jnp.full((PLAN,), load, jnp.int32)
    output = None
    for group in range(KEY_VALUE_HEADS):
        output = attend(everything, queries, group, gather(packed[group]), reply, into=output)
    for section in range(SECTIONS):
        distance = members >> (section + 1)
        hands = hand_counts[0, :, section]
        giving = lax.dynamic_index_in_dim(hands, my_index, keepdims=False)
        getting = lax.dynamic_index_in_dim(hands, my_index ^ distance, keepdims=False)
        keeping = load - giving

        def trade(count, output, keeping, distance=distance):
            if count == 0:
                return output
            top_rows = lax.dynamic_slice_in_dim(
                output, keeping * TILE_TOKENS, count * TILE_TOKENS, 0
            )
            return lax.dynamic_update_slice_in_dim(
                output, swap(top_rows, distance), keeping * TILE_TOKENS, 0
            )

        output = lax.switch(
            jnp.maximum(giving, getting),
            [functools.partial(trade, count) for count in range(HAND + 1)],
            output,
            keeping,
        )
        load = keeping + getting
    return output


def per_device(
    queries, prompt_keys, prompt_value_rows, reply_keys, response_values, lengths, hand_counts
):
    plan, choice = make_plan(lax.axis_size("sample"), lengths, hand_counts)
    packed = [
        jnp.concatenate(
            [
                array[0, :, group * HEAD_WIDTH : (group + 1) * HEAD_WIDTH]
                for array in (prompt_keys, prompt_value_rows)
            ],
            axis=1,
        )
        for group in range(KEY_VALUE_HEADS)
    ]
    output = lax.switch(
        choice[0],
        [functools.partial(run_bundle, bundle) for bundle in BUNDLES] + [run_chain],
        plan,
        queries[0],
        packed,
        (reply_keys[0], response_values[0]),
        lengths,
        hand_counts,
    )
    return output[None]


def solution(mesh):
    placed = (
        P("prompt", "sample", None),
        P("prompt", "sample", None),
        P("prompt", "sample", None),
        P("prompt", "sample", None),
        P("prompt", "sample", None),
        P("prompt", None),
        P("prompt", None, None),
    )
    return jax.shard_map(
        per_device,
        mesh=mesh,
        in_specs=placed,
        out_specs=P("prompt", "sample", None),
        check_vma=False,
    )
```

```python
import functools
import math

import jax
import jax.numpy as jnp
from jax import lax
from jax.experimental import pallas as pl
from jax.experimental.pallas import tpu as pltpu
from jax.sharding import PartitionSpec as P

KEY_VALUE_HEADS = 2
QUERY_PER_KEY = 7
HEAD_WIDTH = 128
TILE_TOKENS = 128
MOST_TILES = 4
SECTIONS = 2
HAND = 2
HEADS = KEY_VALUE_HEADS * QUERY_PER_KEY
COLUMNS = HEADS * HEAD_WIDTH
SCALE = math.log2(math.e) / math.sqrt(HEAD_WIDTH)
MASKED = -1e30
SAFE = 100.0
TRANSPOSED = (((1,), (1,)), ((), ()))
JOBS = tuple(
    (group, head, min(head + 2, QUERY_PER_KEY))
    for group in range(KEY_VALUE_HEADS)
    for head in range(0, QUERY_PER_KEY, 2)
)

FAR = ((0, 2), (2, 0), (1, 3), (3, 1))
NEAR = ((0, 1), (1, 0), (2, 3), (3, 2))
CROSS = ((0, 3), (3, 0), (1, 2), (2, 1))


def usual_bundles():
    bundles = []
    for onward in (True, False):
        for beside in ((), ((1, 3),), ((3, 1),)):
            for more in ((), ((0, 1),), ((1, 0),), ((3, 0),)):
                far = ((0, 2),) + beside
                if not onward:
                    bundle = (far, ((0, 2),)) + ((more,) if more else ())
                elif more == ((3, 0),):
                    bundle = (far, ((0, 3), (3, 0)))
                else:
                    bundle = (far, ((0, 3),)) + ((more,) if more else ())
                bundles.append(bundle)
    return sorted(bundles, key=lambda bundle: (len(bundle), sum(map(len, bundle))))


BUNDLES = (
    *usual_bundles(),
    (((0, 2), (1, 3)), ((0, 2), (1, 3))),
    (((0, 2), (3, 1)), ((0, 2), (3, 1)), ((0, 3), (3, 0))),
    (FAR, FAR, CROSS, NEAR),
)
PERMUTES = max(len(bundle) for bundle in BUNDLES)
SEND, FILL, KEPT = 0, PERMUTES, 2 * PERMUTES
LIVE = KEPT + 1
TRADED = LIVE + 1
KEEPING = TRADED + SECTIONS
PLAN = KEEPING + SECTIONS


def bundle_entries(bundle):
    entries, capacity = [], {}
    for permute in bundle:
        (distance,) = {source ^ target for source, target in permute}
        turn = sum(1 for other, _ in entries if other == distance)
        entries.append((distance, turn))
        for source, _ in permute:
            assert capacity.get((source, distance), 0) == turn
            capacity[source, distance] = turn + 1
    return entries, capacity


def plan_body(members, lengths_ref, hands_ref, plan_ref, choice_ref):
    me = lax.axis_index("sample")
    far, near = members // 2, members // 4

    def counts(device):
        partner = device ^ far
        first = hands_ref[0, 0, device]
        through = jnp.minimum(hands_ref[0, 1, partner], first)
        second = jnp.maximum(hands_ref[0, 1, device] - hands_ref[0, 0, partner], 0)
        return {1: second, 2: first - through, 3: through}

    needs = {}
    for device in range(members):
        for distance, count in counts(device).items():
            key = (device // near, distance)
            needs[key] = jnp.maximum(needs[key], count) if key in needs else count
    choice = jnp.int32(len(BUNDLES))
    for number in reversed(range(len(BUNDLES))):
        _, capacity = bundle_entries(BUNDLES[number])
        lacking = jnp.int32(0)
        for key, count in needs.items():
            lacking = lacking + jnp.maximum(count - capacity.get(key, 0), 0)
        choice = jnp.where(lacking == 0, number, choice)
    choice_ref[0] = choice

    mine = counts(me)
    length = lengths_ref[0, me]
    kept = length - mine[1] - mine[2] - mine[3]
    arriving = {2: counts(me ^ far)[2], 1: counts(me ^ near)[1], 3: counts(me ^ far ^ near)[3]}
    first_tile, first_slot = {}, {}
    tile = slot = kept
    for distance in (1, 2, 3):
        first_tile[distance] = tile
        tile = tile + mine[distance]
    for distance in (2, 1, 3):
        first_slot[distance] = slot
        slot = slot + arriving[distance]
    for index in range(PERMUTES):
        send = fill = jnp.int32(-1)
        for number, bundle in enumerate(BUNDLES):
            entries, _ = bundle_entries(bundle)
            if index < len(entries):
                distance, turn = entries[index]
                here = choice == number
                leaves = jnp.where(turn < mine[distance], first_tile[distance] + turn, -1)
                enters = jnp.where(turn < arriving[distance], first_slot[distance] + turn, -1)
                send = jnp.where(here, leaves, send)
                fill = jnp.where(here, enters, fill)
        plan_ref[SEND + index] = send
        plan_ref[FILL + index] = fill
    plan_ref[KEPT] = jnp.where(choice == len(BUNDLES), length, kept)
    plan_ref[LIVE] = length
    load = length
    for section in range(SECTIONS):
        giving = hands_ref[0, section, me]
        getting = hands_ref[0, section, me ^ (members >> (section + 1))]
        plan_ref[TRADED + section] = jnp.maximum(giving, getting)
        plan_ref[KEEPING + section] = load - giving
        load = load - giving + getting


def make_plan(members, lengths, hand_counts):
    in_smem = pl.BlockSpec(memory_space=pltpu.SMEM)
    by_section = pltpu.with_memory_space_constraint(jnp.swapaxes(hand_counts, 1, 2), pltpu.HBM)
    return pl.pallas_call(
        functools.partial(plan_body, members),
        in_specs=[in_smem, in_smem],
        out_specs=(in_smem, in_smem),
        out_shape=(
            jax.ShapeDtypeStruct((PLAN,), jnp.int32),
            jax.ShapeDtypeStruct((1,), jnp.int32),
        ),
        compiler_params=pltpu.CompilerParams(vmem_limit_bytes=1 << 20),
    )(lengths, by_section)


def head_columns(group, head):
    first = (group * QUERY_PER_KEY + head) * HEAD_WIDTH
    return slice(first, first + HEAD_WIDTH)


def attend_tile(tile, query_ref, blocks, reply, with_max, done):
    peak = [jnp.zeros((8, HEAD_WIDTH), jnp.float32)]

    def score(job):
        group, first, last = job
        columns = slice(group * HEAD_WIDTH, (group + 1) * HEAD_WIDTH)
        rows = jnp.concatenate(
            [query_ref[:, head_columns(group, head)] for head in range(first, last)], axis=0
        )
        scores = []
        for keys, _ in blocks + ([reply] if reply is not None else []):
            block = lax.dot_general(
                rows, keys[:, columns], TRANSPOSED, preferred_element_type=jnp.float32
            )
            if not with_max:
                size = jnp.abs(block).reshape(-1, 8, block.shape[1])
                size = jnp.max(size, axis=0)
                if block.shape[1] % HEAD_WIDTH:
                    size = jnp.max(size, axis=1, keepdims=True)
                width = min(size.shape[1], HEAD_WIDTH)
                for start in range(0, size.shape[1], width):
                    peak[0] = jnp.maximum(peak[0], size[:, start : start + width])
            scores.append(block)
        if reply is not None:
            shape = (TILE_TOKENS, scores[-1].shape[1])
            ahead = lax.broadcasted_iota(jnp.int32, shape, 1) - lax.broadcasted_iota(
                jnp.int32, shape, 0
            )
            bias = jnp.where(ahead <= tile * TILE_TOKENS, 0.0, MASKED)
            scores[-1] = scores[-1] + jnp.concatenate([bias] * (last - first), axis=0)
        return scores

    def finish(job, scores):
        group, first, last = job
        columns = slice(group * HEAD_WIDTH, (group + 1) * HEAD_WIDTH)
        if with_max:
            top = functools.reduce(
                jnp.maximum, [jnp.max(block, axis=1, keepdims=True) for block in scores]
            )
            scores = [block - top for block in scores]
        mix = 0.0
        for block, (_, value) in zip(scores, blocks + ([reply] if reply is not None else [])):
            weights = jnp.exp2(block * SCALE).astype(jnp.bfloat16)
            value = jnp.concatenate(
                [value[:, columns], jnp.ones((value.shape[0], HEAD_WIDTH), jnp.bfloat16)], axis=1
            )
            mix = mix + jnp.dot(weights, value, preferred_element_type=jnp.float32)
        for head in range(first, last):
            part = slice((head - first) * TILE_TOKENS, (head - first + 1) * TILE_TOKENS)
            index = group * QUERY_PER_KEY + head
            done(index, head_columns(group, head), mix[part, :HEAD_WIDTH], mix[part, HEAD_WIDTH:])

    ahead = score(JOBS[0])
    for number, job in enumerate(JOBS):
        scores = ahead
        if number + 1 < len(JOBS):
            ahead = score(JOBS[number + 1])
        finish(job, scores)
    return peak[0]


def rows_of(tile):
    return pl.ds(pl.multiple_of(tile * TILE_TOKENS, TILE_TOKENS), TILE_TOKENS)


def first_body(lengths_ref, query_ref, *refs):
    sources, refs = refs[:4], refs[4:]
    held_ref, mix_ref, total_ref, peak_ref, *targets, block_sems, tile_sems = refs
    length = lengths_ref[0, lax.axis_index("sample")]

    def fetch(tile):
        rows = rows_of(tile)
        return pltpu.make_async_copy(query_ref.at[rows], held_ref.at[rows], tile_sems.at[tile])

    copies = [
        pltpu.make_async_copy(source, target, block_sems.at[number])
        for number, (source, target) in enumerate(zip(sources, targets))
    ]
    fetch(0).start()
    for copy in copies:
        copy.start()

    @pl.loop(1, length)
    def _(tile):
        fetch(tile).start()

    for copy in copies:
        copy.wait()
    own, reply = tuple(targets[:2]), tuple(targets[2:])

    @pl.loop(0, length)
    def _(tile):
        fetch(tile).wait()
        attend_part(tile, held_ref, [own], reply, None, (mix_ref, total_ref, peak_ref))


def next_body(pieces, lengths_ref, query_ref, *refs):
    blocks = list(zip(refs[: 2 * pieces : 2], refs[1 : 2 * pieces : 2]))
    state, target = refs[2 * pieces : 2 * pieces + 3], refs[2 * pieces + 3 :]

    @pl.loop(0, lengths_ref[0, lax.axis_index("sample")])
    def _(tile):
        attend_part(tile, query_ref, blocks, None, state, target)


def attend_part(tile, query_ref, blocks, reply, state, target):
    rows, peak_rows = rows_of(tile), pl.ds(pl.multiple_of(tile * 8, 8), 8)
    mix_ref, total_ref, peak_ref = target
    lanes = lax.broadcasted_iota(jnp.int32, (TILE_TOKENS, HEAD_WIDTH), 1)
    totals = [jnp.zeros((TILE_TOKENS, HEAD_WIDTH), jnp.float32)]

    def done(index, where, mix, total):
        mix_ref[rows, where] = mix if state is None else mix + state[0][rows, where]
        totals[0] = jnp.where(lanes == index, total, totals[0])

    peak = attend_tile(tile, query_ref.at[rows], blocks, reply, False, done)
    total_ref[rows] = totals[0] if state is None else totals[0] + state[1][rows]
    peak_ref[peak_rows] = peak if state is None else jnp.maximum(peak, state[2][peak_rows])


def last_body(pieces, others, plan_ref, query_ref, *refs):
    refs = list(refs)
    blocks = [(refs.pop(0), refs.pop(0)) for _ in range(pieces)]
    mix_ref, total_ref, peak_ref = (refs.pop(0) for _ in range(3))
    far_refs = [refs.pop(0) for _ in range(2 * others)]
    output_ref = refs.pop(0)
    send_refs = [refs.pop(0) for _ in range(PERMUTES)]
    held_ref, zero_ref = refs.pop(0), refs.pop(0)
    near_refs = [refs.pop(0) for _ in range(2 * others)]
    (tile_sems,) = refs
    tiles = output_ref.shape[0] // TILE_TOKENS
    kept = plan_ref[KEPT]

    def put(tile, source):
        return pltpu.make_async_copy(source, output_ref.at[rows_of(tile)], tile_sems.at[tile])

    zero_ref[...] = jnp.zeros(zero_ref.shape, zero_ref.dtype)

    @pl.loop(kept, tiles)
    def _(tile):
        put(tile, zero_ref).start()

    @pl.loop(0, plan_ref[LIVE])
    def _(tile):
        rows, peak_rows = rows_of(tile), pl.ds(pl.multiple_of(tile * 8, 8), 8)

        def done(index, where, mix, total):
            total = total + total_ref[rows, index : index + 1]
            held_ref[rows, where] = ((mix + mix_ref[rows, where]) * (1.0 / total)).astype(
                jnp.bfloat16
            )

        peak = attend_tile(tile, query_ref.at[rows], blocks, None, False, done)
        peak = jnp.max(jnp.maximum(peak, peak_ref[peak_rows]))

        @pl.when(peak * SCALE > SAFE)
        def _():
            for source, target in zip(far_refs, near_refs):
                pltpu.sync_copy(source, target)
            pairs = list(zip(near_refs[::2], near_refs[1::2]))

            def done(index, where, mix, total):
                held_ref[rows, where] = (mix * (1.0 / total)).astype(jnp.bfloat16)

            attend_tile(tile, query_ref.at[rows], blocks + pairs[:-1], pairs[-1], True, done)

        @pl.when(tile < kept)
        def _():
            put(tile, held_ref.at[rows]).start()

        for index, send_ref in enumerate(send_refs):
            @pl.when(plan_ref[SEND + index] == tile)
            def _():
                send_ref[...] = held_ref[rows]

    @pl.loop(0, tiles)
    def _(tile):
        put(tile, zero_ref).wait()


IN_SMEM = pl.BlockSpec(memory_space=pltpu.SMEM)
IN_VMEM = pl.BlockSpec(memory_space=pltpu.VMEM)
ANYWHERE = pl.BlockSpec(memory_space=pl.ANY)


def attend(body, operands, in_specs, out_specs, out_shape, scratch, rows, keys):
    return pl.pallas_call(
        body,
        in_specs=in_specs,
        out_specs=out_specs,
        out_shape=out_shape,
        scratch_shapes=scratch,
        cost_estimate=pl.CostEstimate(
            flops=4 * rows * keys * COLUMNS,
            bytes_accessed=8 * rows * COLUMNS,
            transcendentals=rows * keys * HEADS,
        ),
        compiler_params=pltpu.CompilerParams(vmem_limit_bytes=24 << 20),
    )(*operands)


def state_shapes(rows):
    return [
        pltpu.VMEM((rows, COLUMNS), jnp.float32),
        pltpu.VMEM((rows, HEAD_WIDTH), jnp.float32),
        pltpu.VMEM((rows // TILE_TOKENS * 8, HEAD_WIDTH), jnp.float32),
    ]


def attend_first(lengths, queries, own, reply):
    rows, arrays = queries.shape[0], [*own, *reply]
    queries_here, *state = attend(
        first_body,
        [lengths, queries, *arrays],
        [IN_SMEM] + [ANYWHERE] * 5,
        [IN_VMEM] * 4,
        [pltpu.VMEM(queries.shape, queries.dtype)] + state_shapes(rows),
        [pltpu.VMEM(array.shape, array.dtype) for array in arrays]
        + [pltpu.SemaphoreType.DMA((4,)), pltpu.SemaphoreType.DMA((rows // TILE_TOKENS,))],
        rows,
        own[0].shape[0] + reply[0].shape[0],
    )
    return queries_here, state


def attend_next(lengths, queries, blocks, state):
    rows, arrays = queries.shape[0], [array for block in blocks for array in block]
    return attend(
        functools.partial(next_body, len(blocks)),
        [lengths, queries, *arrays, *state],
        [IN_SMEM] + [IN_VMEM] * (1 + len(arrays) + 3),
        [IN_VMEM] * 3,
        state_shapes(rows),
        [],
        rows,
        sum(block[0].shape[0] for block in blocks),
    )


def attend_last(plan, queries, blocks, others, state):
    rows, arrays = queries.shape[0], [array for block in blocks for array in block]
    earlier = [array for block in others for array in block]
    shape = (TILE_TOKENS, COLUMNS)
    output, *sends = attend(
        functools.partial(last_body, len(blocks), len(others)),
        [plan, queries, *arrays, *state, *earlier],
        [IN_SMEM] + [IN_VMEM] * (1 + len(arrays) + 3) + [ANYWHERE] * len(earlier),
        [ANYWHERE] + [IN_VMEM] * PERMUTES,
        [pltpu.HBM(queries.shape, jnp.bfloat16)] + [pltpu.VMEM(shape, jnp.bfloat16)] * PERMUTES,
        [pltpu.VMEM(queries.shape, jnp.bfloat16), pltpu.VMEM(shape, jnp.bfloat16)]
        + [pltpu.VMEM(array.shape, array.dtype) for array in earlier]
        + [pltpu.SemaphoreType.DMA((rows // TILE_TOKENS,))],
        rows,
        sum(block[0].shape[0] for block in blocks),
    )
    return output, sends


def assemble_body(permutes, plan_ref, *refs):
    arrived, output, semaphores = refs[:permutes], refs[-2], refs[-1]
    copies = []
    for number in range(permutes):
        slot = plan_ref[FILL + number]
        first = pl.multiple_of(jnp.maximum(slot, 0) * TILE_TOKENS, TILE_TOKENS)
        copy = pltpu.make_async_copy(
            arrived[number], output.at[pl.ds(first, TILE_TOKENS)], semaphores.at[number]
        )
        copies.append((slot >= 0, copy))
    for taken, copy in copies:
        pl.when(taken)(copy.start)
    for taken, copy in copies:
        pl.when(taken)(copy.wait)


def assemble(plan, arrived, output, unused):
    return pl.pallas_call(
        functools.partial(assemble_body, len(arrived)),
        in_specs=[IN_SMEM] + [IN_VMEM] * len(arrived) + [ANYWHERE] * (1 + len(unused)),
        out_specs=ANYWHERE,
        out_shape=pltpu.HBM(output.shape, output.dtype),
        scratch_shapes=[pltpu.SemaphoreType.DMA((max(len(arrived), 1),))],
        input_output_aliases={len(arrived) + 1: 0},
        compiler_params=pltpu.CompilerParams(vmem_limit_bytes=1 << 20),
    )(plan, *arrived, output, *unused)


def swap(value, distance):
    members = lax.axis_size("sample")
    return lax.ppermute(value, "sample", [(source, source ^ distance) for source in range(members)])


def gather(own):
    held = [own]
    distance = lax.axis_size("sample") // 2
    while distance:
        held += [tuple(swap(array, distance) for array in block) for block in held]
        distance //= 2
    return held


def run_bundle(bundle, plan, output, sends):
    plan, output, sends = lax.optimization_barrier((plan, output, sends))
    quarter = lax.axis_size("sample") // 4
    arrived = []
    for permute, tile in zip(bundle, sends):
        pairs = [
            (source * quarter + low, target * quarter + low)
            for source, target in permute
            for low in range(quarter)
        ]
        arrived.append(lax.ppermute(tile, "sample", pairs))
    return assemble(plan, arrived, output, sends[len(bundle) :])


def run_chain(plan, output, sends):
    plan, output, sends = lax.optimization_barrier((plan, output, sends))
    output = assemble(plan, [], output, sends)
    for section in range(SECTIONS):
        distance = lax.axis_size("sample") >> (section + 1)

        def trade(count, output, keeping, distance=distance):
            if count == 0:
                return output
            top_rows = lax.dynamic_slice_in_dim(
                output, keeping * TILE_TOKENS, count * TILE_TOKENS, 0
            )
            return lax.dynamic_update_slice_in_dim(
                output, swap(top_rows, distance), keeping * TILE_TOKENS, 0
            )

        output = lax.switch(
            plan[TRADED + section],
            [functools.partial(trade, count) for count in range(HAND + 1)],
            output,
            plan[KEEPING + section],
        )
    return output


def per_device(
    queries, prompt_keys, prompt_value_rows, reply_keys, response_values, lengths, hand_counts
):
    members = lax.axis_size("sample")
    held = gather((prompt_keys[0], prompt_value_rows[0]))
    queries, *own = (
        pltpu.with_memory_space_constraint(array[0], pltpu.HBM)
        for array in (queries, prompt_keys, prompt_value_rows, reply_keys, response_values)
    )
    own, reply = tuple(own[:2]), tuple(own[2:])
    lengths = pltpu.with_memory_space_constraint(lengths, pltpu.HBM)
    held[0] = own
    half = members // 2 + 1
    queries, state = attend_first(lengths, queries, own, reply)
    state = attend_next(lengths, queries, held[1:half], state)
    plan, choice = make_plan(members, lengths, hand_counts)
    output, sends = attend_last(plan, queries, held[half:], held[:half] + [reply], state)
    output = lax.switch(
        choice[0],
        [functools.partial(run_bundle, bundle) for bundle in BUNDLES] + [run_chain],
        plan,
        output,
        sends,
    )
    return output[None]


def solution(mesh):
    placed = (
        P("prompt", "sample", None),
        P("prompt", "sample", None),
        P("prompt", "sample", None),
        P("prompt", "sample", None),
        P("prompt", "sample", None),
        P("prompt", None),
        P("prompt", None, None),
    )
    return jax.shard_map(
        per_device,
        mesh=mesh,
        in_specs=placed,
        out_specs=P("prompt", "sample", None),
        check_vma=False,
    )
```

```python
import functools
import math

import jax
import jax.numpy as jnp
from jax import lax
from jax.experimental import pallas as pl
from jax.experimental.pallas import tpu as pltpu
from jax.sharding import PartitionSpec as P

KEY_VALUE_HEADS = 2
QUERY_PER_KEY = 7
HEAD_WIDTH = 128
TILE_TOKENS = 128
MOST_TILES = 4
SECTIONS = 2
HAND = 2
HEADS = KEY_VALUE_HEADS * QUERY_PER_KEY
COLUMNS = HEADS * HEAD_WIDTH
SCALE = math.log2(math.e) / math.sqrt(HEAD_WIDTH)
MASKED = -1e30
QUERIES, KEYS, SCORES = slice(0, 8), slice(8, 16), slice(16, 24)
SAFE = 100.0
TRANSPOSED = (((1,), (1,)), ((), ()))
def jobs(heads):
    return tuple(
        (group, head, min(head + heads, QUERY_PER_KEY))
        for group in range(KEY_VALUE_HEADS)
        for head in range(0, QUERY_PER_KEY, heads)
    )


FAR = ((0, 2), (2, 0), (1, 3), (3, 1))
NEAR = ((0, 1), (1, 0), (2, 3), (3, 2))
CROSS = ((0, 3), (3, 0), (1, 2), (2, 1))


def usual_bundles():
    bundles = []
    for onward in (True, False):
        for beside in ((), ((1, 3),), ((3, 1),)):
            for more in ((), ((0, 1),), ((1, 0),), ((3, 0),)):
                far = ((0, 2),) + beside
                if not onward:
                    bundle = (far, ((0, 2),)) + ((more,) if more else ())
                elif more == ((3, 0),):
                    bundle = (far, ((0, 3), (3, 0)))
                else:
                    bundle = (far, ((0, 3),)) + ((more,) if more else ())
                bundles.append(bundle)
    return sorted(bundles, key=lambda bundle: (len(bundle), sum(map(len, bundle))))


BUNDLES = (
    *usual_bundles(),
    (((0, 2), (1, 3)), ((0, 2), (1, 3))),
    (((0, 2), (3, 1)), ((0, 2), (3, 1)), ((0, 3), (3, 0))),
    (FAR, FAR, CROSS, NEAR),
)
PERMUTES = max(len(bundle) for bundle in BUNDLES)
SEND, FILL, KEPT = 0, PERMUTES, 2 * PERMUTES
LIVE = KEPT + 1
TRADED = LIVE + 1
KEEPING = TRADED + SECTIONS
PLAN = KEEPING + SECTIONS


def bundle_entries(bundle):
    entries, capacity = [], {}
    for permute in bundle:
        (distance,) = {source ^ target for source, target in permute}
        turn = sum(1 for other, _ in entries if other == distance)
        entries.append((distance, turn))
        for source, _ in permute:
            assert capacity.get((source, distance), 0) == turn
            capacity[source, distance] = turn + 1
    return entries, capacity


def make_plan(members, lengths_ref, hands_ref, plan_ref, choice_ref):
    me = lax.axis_index("sample")
    far, near = members // 2, members // 4

    def counts(device):
        partner = device ^ far
        first = hands_ref[0, 0, device]
        through = jnp.minimum(hands_ref[0, 1, partner], first)
        second = jnp.maximum(hands_ref[0, 1, device] - hands_ref[0, 0, partner], 0)
        return {1: second, 2: first - through, 3: through}

    needs = {}
    for device in range(members):
        for distance, count in counts(device).items():
            key = (device // near, distance)
            needs[key] = jnp.maximum(needs[key], count) if key in needs else count
    choice = jnp.int32(len(BUNDLES))
    for number in reversed(range(len(BUNDLES))):
        _, capacity = bundle_entries(BUNDLES[number])
        lacking = jnp.int32(0)
        for key, count in needs.items():
            lacking = lacking + jnp.maximum(count - capacity.get(key, 0), 0)
        choice = jnp.where(lacking == 0, number, choice)
    choice_ref[0] = choice

    mine = counts(me)
    length = lengths_ref[0, me]
    kept = length - mine[1] - mine[2] - mine[3]
    arriving = {2: counts(me ^ far)[2], 1: counts(me ^ near)[1], 3: counts(me ^ far ^ near)[3]}
    first_tile, first_slot = {}, {}
    tile = slot = kept
    for distance in (1, 2, 3):
        first_tile[distance] = tile
        tile = tile + mine[distance]
    for distance in (2, 1, 3):
        first_slot[distance] = slot
        slot = slot + arriving[distance]
    for index in range(PERMUTES):
        send = fill = jnp.int32(-1)
        for number, bundle in enumerate(BUNDLES):
            entries, _ = bundle_entries(bundle)
            if index < len(entries):
                distance, turn = entries[index]
                here = choice == number
                leaves = jnp.where(turn < mine[distance], first_tile[distance] + turn, -1)
                enters = jnp.where(turn < arriving[distance], first_slot[distance] + turn, -1)
                send = jnp.where(here, leaves, send)
                fill = jnp.where(here, enters, fill)
        plan_ref[SEND + index] = send
        plan_ref[FILL + index] = fill
    plan_ref[KEPT] = jnp.where(choice == len(BUNDLES), length, kept)
    plan_ref[LIVE] = length
    load = length
    for section in range(SECTIONS):
        giving = hands_ref[0, section, me]
        getting = hands_ref[0, section, me ^ (members >> (section + 1))]
        plan_ref[TRADED + section] = jnp.maximum(giving, getting)
        plan_ref[KEEPING + section] = load - giving
        load = load - giving + getting


def head_columns(group, head):
    first = (group * QUERY_PER_KEY + head) * HEAD_WIDTH
    return slice(first, first + HEAD_WIDTH)


def attend_tile(tile, query_ref, blocks, reply, with_max, done, see=None, heads=QUERY_PER_KEY):
    pairs = blocks + ([reply] if reply is not None else [])

    def score(job):
        group, first, last = job
        columns = slice(group * HEAD_WIDTH, (group + 1) * HEAD_WIDTH)
        rows = jnp.concatenate(
            [query_ref[:, head_columns(group, head)] for head in range(first, last)], axis=0
        )
        scores = [
            lax.dot_general(
                rows, keys[:, columns], TRANSPOSED, preferred_element_type=jnp.float32
            )
            for keys, _ in pairs
        ]
        if see is not None:
            see(rows, scores)
        if reply is not None:
            shape = (TILE_TOKENS, scores[-1].shape[1])
            ahead = lax.broadcasted_iota(jnp.int32, shape, 1) - lax.broadcasted_iota(
                jnp.int32, shape, 0
            )
            bias = jnp.where(ahead <= tile * TILE_TOKENS, 0.0, MASKED)
            scores[-1] = scores[-1] + jnp.concatenate([bias] * (last - first), axis=0)
        return scores

    def finish(job, scores):
        group, first, last = job
        columns = slice(group * HEAD_WIDTH, (group + 1) * HEAD_WIDTH)
        if with_max:
            top = functools.reduce(
                jnp.maximum, [jnp.max(block, axis=1, keepdims=True) for block in scores]
            )
            scores = [block - top for block in scores]
        mix = 0.0
        for block, (_, value) in zip(scores, pairs):
            weights = jnp.exp2(block * SCALE).astype(jnp.bfloat16)
            value = jnp.concatenate(
                [value[:, columns], jnp.ones((value.shape[0], HEAD_WIDTH), jnp.bfloat16)], axis=1
            )
            mix = mix + jnp.dot(weights, value, preferred_element_type=jnp.float32)
        for head in range(first, last):
            part = slice((head - first) * TILE_TOKENS, (head - first + 1) * TILE_TOKENS)
            index = group * QUERY_PER_KEY + head
            done(index, head_columns(group, head), mix[part, :HEAD_WIDTH], mix[part, HEAD_WIDTH:])

    turns = jobs(heads)
    ahead = score(turns[0])
    for number, job in enumerate(turns):
        scores = ahead
        if number + 1 < len(turns):
            ahead = score(turns[number + 1])
        finish(job, scores)


def rows_of(tile):
    return pl.ds(pl.multiple_of(tile * TILE_TOKENS, TILE_TOKENS), TILE_TOKENS)


def largest_square(rows):
    rows = rows.astype(jnp.float32)
    squares = jnp.sum(rows * rows, axis=1, keepdims=True)
    squares = jnp.max(squares.reshape(-1, 8, 1), axis=0)
    return jnp.broadcast_to(squares, (8, HEAD_WIDTH))


def largest_key_square(blocks):
    return functools.reduce(
        jnp.maximum,
        [
            largest_square(keys[:, group * HEAD_WIDTH : (group + 1) * HEAD_WIDTH])
            for keys, _ in blocks
            for group in range(KEY_VALUE_HEADS)
        ],
    )


def first_body(members, lengths_ref, hands_ref, query_ref, *refs):
    sources, refs = refs[:4], refs[4:]
    plan_ref, choice_ref, held_ref, mix_ref, total_ref, size_ref, *targets = refs
    targets, (block_sems, tile_sems) = targets[:4], targets[4:]
    length = lengths_ref[0, lax.axis_index("sample")]

    def fetch(tile):
        rows = rows_of(tile)
        return pltpu.make_async_copy(query_ref.at[rows], held_ref.at[rows], tile_sems.at[tile])

    copies = [
        pltpu.make_async_copy(source, target, block_sems.at[number])
        for number, (source, target) in enumerate(zip(sources, targets))
    ]
    fetch(0).start()
    for copy in copies:
        copy.start()

    @pl.loop(1, length)
    def _(tile):
        fetch(tile).start()

    make_plan(members, lengths_ref, hands_ref, plan_ref, choice_ref)
    for copy in copies:
        copy.wait()
    own, reply = tuple(targets[:2]), tuple(targets[2:])
    size_ref[QUERIES] = jnp.zeros((8, HEAD_WIDTH), jnp.float32)
    size_ref[KEYS] = largest_key_square([own, reply])
    size_ref[SCORES] = jnp.zeros((8, HEAD_WIDTH), jnp.float32)

    @pl.loop(0, length)
    def _(tile):
        fetch(tile).wait()
        largest = [size_ref[QUERIES]]

        def see(rows, scores):
            largest[0] = jnp.maximum(largest[0], largest_square(rows))

        attend_part(tile, held_ref, [own], reply, None, (mix_ref, total_ref), see)
        size_ref[QUERIES] = largest[0]


def next_body(pieces, lengths_ref, query_ref, *refs):
    blocks = list(zip(refs[: 2 * pieces : 2], refs[1 : 2 * pieces : 2]))
    state, target = refs[2 * pieces : 2 * pieces + 3], refs[2 * pieces + 3 :]
    size_ref = target[2]
    size_ref[...] = state[2][...]

    @pl.loop(0, lengths_ref[0, lax.axis_index("sample")])
    def _(tile):
        largest = [size_ref[SCORES]]

        def see(rows, scores):
            for block in scores:
                size = jnp.max(jnp.abs(block).reshape(-1, 8, block.shape[1]), axis=0)
                if block.shape[1] % HEAD_WIDTH:
                    size = jnp.max(size, axis=1, keepdims=True)
                width = min(size.shape[1], HEAD_WIDTH)
                for start in range(0, size.shape[1], width):
                    largest[0] = jnp.maximum(largest[0], size[:, start : start + width])

        attend_part(tile, query_ref, blocks, None, state, target, see)
        size_ref[SCORES] = largest[0]


def attend_part(tile, query_ref, blocks, reply, state, target, see=None):
    rows = rows_of(tile)
    mix_ref, total_ref = target[:2]
    lanes = lax.broadcasted_iota(jnp.int32, (TILE_TOKENS, HEAD_WIDTH), 1)
    totals = [jnp.zeros((TILE_TOKENS, HEAD_WIDTH), jnp.float32)]

    def done(index, where, mix, total):
        mix_ref[rows, where] = mix if state is None else mix + state[0][rows, where]
        totals[0] = jnp.where(lanes == index, total, totals[0])

    attend_tile(
        tile, query_ref.at[rows], blocks, reply, False, done, see, 2 if reply else QUERY_PER_KEY
    )
    total_ref[rows] = totals[0] if state is None else totals[0] + state[1][rows]


def finish_tile(tile, query_ref, blocks, mix_ref, total_ref, held_ref):
    rows = rows_of(tile)

    def done(index, where, mix, total):
        total = total + total_ref[rows, index : index + 1]
        held_ref[rows, where] = ((mix + mix_ref[rows, where]) * (1.0 / total)).astype(jnp.bfloat16)

    attend_tile(tile, query_ref.at[rows], blocks, None, False, done)


def last_body(pieces, others, plan_ref, query_ref, *refs):
    refs = list(refs)
    blocks = [(refs.pop(0), refs.pop(0)) for _ in range(pieces)]
    mix_ref, total_ref, size_ref = (refs.pop(0) for _ in range(3))
    far_refs = [refs.pop(0) for _ in range(2 * others)]
    size_out_ref, held_ref = refs.pop(0), refs.pop(0)
    send_refs = [refs.pop(0) for _ in range(PERMUTES)]
    near_refs = refs
    kept, live = plan_ref[KEPT], plan_ref[LIVE]
    keys = jnp.maximum(size_ref[KEYS], largest_key_square(blocks))
    squares = jnp.max(size_ref[QUERIES], axis=0, keepdims=True) * jnp.max(keys, axis=0, keepdims=True)
    size = jnp.maximum(jnp.sqrt(squares), jnp.max(size_ref[SCORES], axis=0, keepdims=True))
    size_out_ref[...] = jnp.broadcast_to(size, size_out_ref.shape)

    @pl.loop(kept, live)
    def _(tile):
        finish_tile(tile, query_ref, blocks, mix_ref, total_ref, held_ref)

    @pl.when(jnp.max(size) * SCALE > SAFE)
    def _():
        for source, target in zip(far_refs, near_refs):
            pltpu.sync_copy(source, target)
        pairs = list(zip(near_refs[::2], near_refs[1::2]))

        @pl.loop(0, live)
        def _(tile):
            rows = rows_of(tile)

            def done(index, where, mix, total):
                held_ref[rows, where] = (mix * (1.0 / total)).astype(jnp.bfloat16)

            attend_tile(tile, query_ref.at[rows], blocks + pairs[:-1], pairs[-1], True, done, heads=2)

    for index, send_ref in enumerate(send_refs):
        tile = plan_ref[SEND + index]

        @pl.when(tile >= 0)
        def _():
            send_ref[...] = held_ref[rows_of(tile)]


def kept_body(pieces, plan_ref, query_ref, *refs):
    refs = list(refs)
    blocks = [(refs.pop(0), refs.pop(0)) for _ in range(pieces)]
    mix_ref, total_ref, size_ref, done_ref, output_ref, held_ref, zero_ref, tile_sems = refs
    tiles = output_ref.shape[0] // TILE_TOKENS
    kept = plan_ref[KEPT]
    waiting = jnp.where(jnp.max(size_ref[...]) * SCALE > SAFE, 0, kept)

    def put(tile, source):
        return pltpu.make_async_copy(source, output_ref.at[rows_of(tile)], tile_sems.at[tile])

    zero_ref[...] = jnp.zeros(zero_ref.shape, zero_ref.dtype)

    @pl.loop(kept, tiles)
    def _(tile):
        put(tile, zero_ref).start()

    @pl.loop(waiting, kept)
    def _(tile):
        put(tile, done_ref.at[rows_of(tile)]).start()

    @pl.loop(0, waiting)
    def _(tile):
        rows = rows_of(tile)

        @pl.loop(0, HEADS)
        def _(head):
            where = pl.ds(pl.multiple_of(head * HEAD_WIDTH, HEAD_WIDTH), HEAD_WIDTH)
            group = head // QUERY_PER_KEY
            columns = pl.ds(pl.multiple_of(group * HEAD_WIDTH, HEAD_WIDTH), HEAD_WIDTH)
            lanes = lax.broadcasted_iota(jnp.int32, (TILE_TOKENS, HEAD_WIDTH), 1)
            total = jnp.sum(jnp.where(lanes == head, total_ref[rows], 0.0), axis=1, keepdims=True)
            mix = mix_ref[rows, where]
            for key_ref, value_ref in blocks:
                weights = lax.dot_general(
                    query_ref[rows, where],
                    key_ref[:, columns],
                    TRANSPOSED,
                    preferred_element_type=jnp.float32,
                )
                weights = jnp.exp2(weights * SCALE).astype(jnp.bfloat16)
                value = value_ref[:, columns]
                value = jnp.concatenate([value, jnp.ones(value.shape, value.dtype)], axis=1)
                more = jnp.dot(weights, value, preferred_element_type=jnp.float32)
                mix, total = mix + more[:, :HEAD_WIDTH], total + more[:, HEAD_WIDTH:]
            held_ref[rows, where] = (mix * (1.0 / total)).astype(jnp.bfloat16)

        put(tile, held_ref.at[rows]).start()

    @pl.loop(0, tiles)
    def _(tile):
        put(tile, zero_ref).wait()


IN_SMEM = pl.BlockSpec(memory_space=pltpu.SMEM)
IN_VMEM = pl.BlockSpec(memory_space=pltpu.VMEM)
ANYWHERE = pl.BlockSpec(memory_space=pl.ANY)


def attend(body, operands, in_specs, out_specs, out_shape, scratch, rows, keys):
    return pl.pallas_call(
        body,
        in_specs=in_specs,
        out_specs=out_specs,
        out_shape=out_shape,
        scratch_shapes=scratch,
        cost_estimate=pl.CostEstimate(
            flops=4 * rows * keys * COLUMNS,
            bytes_accessed=8 * rows * COLUMNS,
            transcendentals=rows * keys * HEADS,
        ),
        compiler_params=pltpu.CompilerParams(vmem_limit_bytes=24 << 20),
    )(*operands)


def state_shapes(rows):
    return [
        pltpu.VMEM((rows, COLUMNS), jnp.float32),
        pltpu.VMEM((rows, HEAD_WIDTH), jnp.float32),
        pltpu.VMEM((24, HEAD_WIDTH), jnp.float32),
    ]


def attend_first(members, lengths, hands, queries, own, reply):
    rows, arrays = queries.shape[0], [*own, *reply]
    plan, choice, queries_here, *state = attend(
        functools.partial(first_body, members),
        [lengths, hands, queries, *arrays],
        [IN_SMEM] * 2 + [ANYWHERE] * 5,
        [IN_SMEM] * 2 + [IN_VMEM] * 4,
        [jax.ShapeDtypeStruct((PLAN,), jnp.int32), jax.ShapeDtypeStruct((1,), jnp.int32)]
        + [pltpu.VMEM(queries.shape, queries.dtype)]
        + state_shapes(rows),
        [pltpu.VMEM(array.shape, array.dtype) for array in arrays]
        + [pltpu.SemaphoreType.DMA((4,)), pltpu.SemaphoreType.DMA((rows // TILE_TOKENS,))],
        rows,
        own[0].shape[0] + reply[0].shape[0],
    )
    return plan, choice, queries_here, state


def attend_next(lengths, queries, blocks, state):
    rows, arrays = queries.shape[0], [array for block in blocks for array in block]
    return attend(
        functools.partial(next_body, len(blocks)),
        [lengths, queries, *arrays, *state],
        [IN_SMEM] + [IN_VMEM] * (1 + len(arrays) + 3),
        [IN_VMEM] * 3,
        state_shapes(rows),
        [],
        rows,
        sum(block[0].shape[0] for block in blocks),
    )


def attend_last(plan, queries, blocks, others, state):
    rows, arrays = queries.shape[0], [array for block in blocks for array in block]
    earlier = [array for block in others for array in block]
    shape = (TILE_TOKENS, COLUMNS)
    size, done, *sends = attend(
        functools.partial(last_body, len(blocks), len(others)),
        [plan, queries, *arrays, *state, *earlier],
        [IN_SMEM] + [IN_VMEM] * (1 + len(arrays) + 3) + [ANYWHERE] * len(earlier),
        [IN_VMEM] * (2 + PERMUTES),
        [pltpu.VMEM((8, HEAD_WIDTH), jnp.float32), pltpu.VMEM(queries.shape, jnp.bfloat16)]
        + [pltpu.VMEM(shape, jnp.bfloat16)] * PERMUTES,
        [pltpu.VMEM(array.shape, array.dtype) for array in earlier],
        rows,
        sum(block[0].shape[0] for block in blocks),
    )
    return size, done, sends


def attend_kept(plan, queries, blocks, state, size, done):
    rows, arrays = queries.shape[0], [array for block in blocks for array in block]
    operands = [plan, queries, *arrays, *state[:2], size, done]
    return attend(
        functools.partial(kept_body, len(blocks)),
        operands,
        [IN_SMEM] + [IN_VMEM] * (len(operands) - 1),
        ANYWHERE,
        pltpu.HBM(queries.shape, jnp.bfloat16),
        [
            pltpu.VMEM(queries.shape, jnp.bfloat16),
            pltpu.VMEM((TILE_TOKENS, COLUMNS), jnp.bfloat16),
            pltpu.SemaphoreType.DMA((rows // TILE_TOKENS,)),
        ],
        rows,
        sum(block[0].shape[0] for block in blocks),
    )


def assemble_body(permutes, plan_ref, *refs):
    arrived, output, semaphores = refs[:permutes], refs[-2], refs[-1]
    copies = []
    for number in range(permutes):
        slot = plan_ref[FILL + number]
        first = pl.multiple_of(jnp.maximum(slot, 0) * TILE_TOKENS, TILE_TOKENS)
        copy = pltpu.make_async_copy(
            arrived[number], output.at[pl.ds(first, TILE_TOKENS)], semaphores.at[number]
        )
        copies.append((slot >= 0, copy))
    for taken, copy in copies:
        pl.when(taken)(copy.start)
    for taken, copy in copies:
        pl.when(taken)(copy.wait)


def assemble(plan, arrived, output, unused):
    return pl.pallas_call(
        functools.partial(assemble_body, len(arrived)),
        in_specs=[IN_SMEM] + [IN_VMEM] * len(arrived) + [ANYWHERE] * (1 + len(unused)),
        out_specs=ANYWHERE,
        out_shape=pltpu.HBM(output.shape, output.dtype),
        scratch_shapes=[pltpu.SemaphoreType.DMA((max(len(arrived), 1),))],
        input_output_aliases={len(arrived) + 1: 0},
        compiler_params=pltpu.CompilerParams(vmem_limit_bytes=1 << 20),
    )(plan, *arrived, output, *unused)


def swap(value, distance):
    members = lax.axis_size("sample")
    return lax.ppermute(value, "sample", [(source, source ^ distance) for source in range(members)])


def gather(own):
    held = [own]
    distance = lax.axis_size("sample") // 2
    while distance:
        held += [tuple(swap(array, distance) for array in block) for block in held]
        distance //= 2
    return held


def run_bundle(bundle, *operands):
    plan, sends, *rest = lax.optimization_barrier(operands)
    quarter = lax.axis_size("sample") // 4
    arrived = []
    for permute, tile in zip(bundle, sends):
        pairs = [
            (source * quarter + low, target * quarter + low)
            for source, target in permute
            for low in range(quarter)
        ]
        arrived.append(lax.ppermute(tile, "sample", pairs))
    output = attend_kept(plan, *rest)
    return assemble(plan, arrived, output, sends[len(bundle) :])


def run_chain(*operands):
    plan, sends, *rest = lax.optimization_barrier(operands)
    output = assemble(plan, [], attend_kept(plan, *rest), sends)
    for section in range(SECTIONS):
        distance = lax.axis_size("sample") >> (section + 1)

        def trade(count, output, keeping, distance=distance):
            if count == 0:
                return output
            top_rows = lax.dynamic_slice_in_dim(
                output, keeping * TILE_TOKENS, count * TILE_TOKENS, 0
            )
            return lax.dynamic_update_slice_in_dim(
                output, swap(top_rows, distance), keeping * TILE_TOKENS, 0
            )

        output = lax.switch(
            plan[TRADED + section],
            [functools.partial(trade, count) for count in range(HAND + 1)],
            output,
            plan[KEEPING + section],
        )
    return output


def per_device(
    queries, prompt_keys, prompt_value_rows, reply_keys, response_values, lengths, hand_counts
):
    members = lax.axis_size("sample")
    held = gather((prompt_keys[0], prompt_value_rows[0]))
    queries, *own = (
        pltpu.with_memory_space_constraint(array[0], pltpu.HBM)
        for array in (queries, prompt_keys, prompt_value_rows, reply_keys, response_values)
    )
    own, reply = tuple(own[:2]), tuple(own[2:])
    lengths = pltpu.with_memory_space_constraint(lengths, pltpu.HBM)
    held[0] = own
    half = members // 2 + 1
    hands = pltpu.with_memory_space_constraint(jnp.swapaxes(hand_counts, 1, 2), pltpu.HBM)
    plan, choice, queries, state = attend_first(members, lengths, hands, queries, own, reply)
    state = attend_next(lengths, queries, held[1:half], state)
    size, done, sends = attend_last(plan, queries, held[half:], held[:half] + [reply], state)
    output = lax.switch(
        choice[0],
        [functools.partial(run_bundle, bundle) for bundle in BUNDLES] + [run_chain],
        plan,
        sends,
        queries,
        held[half:],
        state,
        size,
        done,
    )
    return output[None]


def solution(mesh):
    placed = (
        P("prompt", "sample", None),
        P("prompt", "sample", None),
        P("prompt", "sample", None),
        P("prompt", "sample", None),
        P("prompt", "sample", None),
        P("prompt", None),
        P("prompt", None, None),
    )
    return jax.shard_map(
        per_device,
        mesh=mesh,
        in_specs=placed,
        out_specs=P("prompt", "sample", None),
        check_vma=False,
    )
```

```python
import functools
import math

import jax
import jax.numpy as jnp
from jax import lax
from jax.experimental import pallas as pl
from jax.experimental.pallas import tpu as pltpu
from jax.sharding import PartitionSpec as P

KEY_VALUE_HEADS = 2
QUERY_PER_KEY = 7
HEAD_WIDTH = 128
TILE_TOKENS = 128
MOST_TILES = 4
SECTIONS = 2
HAND = 2
HEADS = KEY_VALUE_HEADS * QUERY_PER_KEY
COLUMNS = HEADS * HEAD_WIDTH
SCALE = math.log2(math.e) / math.sqrt(HEAD_WIDTH)
MASKED = -1e30
QUERIES, KEYS, SCORES = slice(0, 8), slice(8, 16), slice(16, 24)
SAFE = 100.0
TRANSPOSED = (((1,), (1,)), ((), ()))
def jobs(heads):
    return tuple(
        (group, head, min(head + heads, QUERY_PER_KEY))
        for group in range(KEY_VALUE_HEADS)
        for head in range(0, QUERY_PER_KEY, heads)
    )


FAR = ((0, 2), (2, 0), (1, 3), (3, 1))
NEAR = ((0, 1), (1, 0), (2, 3), (3, 2))
CROSS = ((0, 3), (3, 0), (1, 2), (2, 1))


def usual_bundles():
    trades = {
        (): ((), ((0, 1),), ((1, 0),), ((3, 0),)),
        ((1, 3),): ((), ((0, 1),), ((1, 0),)),
        ((3, 1),): ((), ((3, 0),)),
    }
    bundles = []
    for beside, others in trades.items():
        for more in others:
            far, onward = ((0, 2),) + beside, ((0, 3),)
            bundles.append((far, ((0, 2),)) + ((more,) if more else ()))
            if more == ((3, 0),):
                bundles.append((far, onward + more))
            else:
                bundles.append((far, onward) + ((more,) if more else ()))
    return sorted(bundles, key=lambda bundle: (len(bundle), sum(map(len, bundle))))


BUNDLES = (
    *usual_bundles(),
    (((0, 2), (1, 3)), ((0, 2), (1, 3))),
    (((0, 2), (3, 1)), ((0, 2), (3, 1)), ((0, 3), (3, 0))),
    (FAR, FAR, CROSS, NEAR),
)
PERMUTES = max(len(bundle) for bundle in BUNDLES)
SEND, FILL, KEPT = 0, PERMUTES, 2 * PERMUTES
LIVE = KEPT + 1
TRADED = LIVE + 1
KEEPING = TRADED + SECTIONS
PLAN = KEEPING + SECTIONS


def bundle_entries(bundle):
    entries, capacity = [], {}
    for permute in bundle:
        (distance,) = {source ^ target for source, target in permute}
        turn = sum(1 for other, _ in entries if other == distance)
        entries.append((distance, turn))
        for source, _ in permute:
            assert capacity.get((source, distance), 0) == turn
            capacity[source, distance] = turn + 1
    return entries, capacity


def make_plan(members, lengths_ref, hands_ref, plan_ref, choice_ref):
    me = lax.axis_index("sample")
    far, near = members // 2, members // 4

    def counts(device):
        partner = device ^ far
        first = hands_ref[0, 0, device]
        through = jnp.minimum(hands_ref[0, 1, partner], first)
        second = jnp.maximum(hands_ref[0, 1, device] - hands_ref[0, 0, partner], 0)
        return {1: second, 2: first - through, 3: through}

    needs = {}
    for device in range(members):
        for distance, count in counts(device).items():
            key = (device // near, distance)
            needs[key] = jnp.maximum(needs[key], count) if key in needs else count
    choice = jnp.int32(len(BUNDLES))
    for number in reversed(range(len(BUNDLES))):
        _, capacity = bundle_entries(BUNDLES[number])
        lacking = jnp.int32(0)
        for key, count in needs.items():
            lacking = lacking + jnp.maximum(count - capacity.get(key, 0), 0)
        choice = jnp.where(lacking == 0, number, choice)
    choice_ref[0] = choice

    mine = counts(me)
    length = lengths_ref[0, me]
    kept = length - mine[1] - mine[2] - mine[3]
    arriving = {2: counts(me ^ far)[2], 1: counts(me ^ near)[1], 3: counts(me ^ far ^ near)[3]}
    first_tile, first_slot = {}, {}
    tile = slot = kept
    for distance in (1, 2, 3):
        first_tile[distance] = tile
        tile = tile + mine[distance]
    for distance in (2, 1, 3):
        first_slot[distance] = slot
        slot = slot + arriving[distance]
    for index in range(PERMUTES):
        send = fill = jnp.int32(-1)
        for number, bundle in enumerate(BUNDLES):
            entries, _ = bundle_entries(bundle)
            if index < len(entries):
                distance, turn = entries[index]
                here = choice == number
                leaves = jnp.where(turn < mine[distance], first_tile[distance] + turn, -1)
                enters = jnp.where(turn < arriving[distance], first_slot[distance] + turn, -1)
                send = jnp.where(here, leaves, send)
                fill = jnp.where(here, enters, fill)
        plan_ref[SEND + index] = send
        plan_ref[FILL + index] = fill
    plan_ref[KEPT] = jnp.where(choice == len(BUNDLES), length, kept)
    plan_ref[LIVE] = length
    load = length
    for section in range(SECTIONS):
        giving = hands_ref[0, section, me]
        getting = hands_ref[0, section, me ^ (members >> (section + 1))]
        plan_ref[TRADED + section] = jnp.maximum(giving, getting)
        plan_ref[KEEPING + section] = load - giving
        load = load - giving + getting


def head_columns(group, head):
    first = (group * QUERY_PER_KEY + head) * HEAD_WIDTH
    return slice(first, first + HEAD_WIDTH)


def attend_tile(tile, query_ref, blocks, reply, with_max, done, see=None, heads=QUERY_PER_KEY):
    pairs = blocks + ([reply] if reply is not None else [])

    def score(job):
        group, first, last = job
        columns = slice(group * HEAD_WIDTH, (group + 1) * HEAD_WIDTH)
        rows = jnp.concatenate(
            [query_ref[:, head_columns(group, head)] for head in range(first, last)], axis=0
        )
        scores = [
            lax.dot_general(
                rows, keys[:, columns], TRANSPOSED, preferred_element_type=jnp.float32
            )
            for keys, _ in pairs
        ]
        if see is not None:
            see(rows, scores)
        if reply is not None:
            shape = (TILE_TOKENS, scores[-1].shape[1])
            ahead = lax.broadcasted_iota(jnp.int32, shape, 1) - lax.broadcasted_iota(
                jnp.int32, shape, 0
            )
            bias = jnp.where(ahead <= tile * TILE_TOKENS, 0.0, MASKED)
            scores[-1] = scores[-1] + jnp.concatenate([bias] * (last - first), axis=0)
        return scores

    def finish(job, scores):
        group, first, last = job
        columns = slice(group * HEAD_WIDTH, (group + 1) * HEAD_WIDTH)
        if with_max:
            top = functools.reduce(
                jnp.maximum, [jnp.max(block, axis=1, keepdims=True) for block in scores]
            )
            scores = [block - top for block in scores]
        mix = 0.0
        for block, (_, value) in zip(scores, pairs):
            weights = jnp.exp2(block * SCALE).astype(jnp.bfloat16)
            value = jnp.concatenate(
                [value[:, columns], jnp.ones((value.shape[0], HEAD_WIDTH), jnp.bfloat16)], axis=1
            )
            mix = mix + jnp.dot(weights, value, preferred_element_type=jnp.float32)
        for head in range(first, last):
            part = slice((head - first) * TILE_TOKENS, (head - first + 1) * TILE_TOKENS)
            index = group * QUERY_PER_KEY + head
            done(index, head_columns(group, head), mix[part, :HEAD_WIDTH], mix[part, HEAD_WIDTH:])

    turns = jobs(heads)
    ahead = score(turns[0])
    for number, job in enumerate(turns):
        scores = ahead
        if number + 1 < len(turns):
            ahead = score(turns[number + 1])
        finish(job, scores)


def rows_of(tile):
    return pl.ds(pl.multiple_of(tile * TILE_TOKENS, TILE_TOKENS), TILE_TOKENS)


def largest_square(rows):
    rows = rows.astype(jnp.float32)
    squares = jnp.sum(rows * rows, axis=1, keepdims=True)
    squares = jnp.max(squares.reshape(-1, 8, 1), axis=0)
    return jnp.broadcast_to(squares, (8, HEAD_WIDTH))


def largest_key_square(blocks):
    return functools.reduce(
        jnp.maximum,
        [
            largest_square(keys[:, group * HEAD_WIDTH : (group + 1) * HEAD_WIDTH])
            for keys, _ in blocks
            for group in range(KEY_VALUE_HEADS)
        ],
    )


def first_body(members, lengths_ref, hands_ref, query_ref, *refs):
    sources, refs = refs[:4], refs[4:]
    plan_ref, choice_ref, held_ref, mix_ref, total_ref, size_ref, *targets = refs
    targets, (block_sems, tile_sems) = targets[:4], targets[4:]
    length = lengths_ref[0, lax.axis_index("sample")]

    def fetch(tile):
        rows = rows_of(tile)
        return pltpu.make_async_copy(query_ref.at[rows], held_ref.at[rows], tile_sems.at[tile])

    copies = [
        pltpu.make_async_copy(source, target, block_sems.at[number])
        for number, (source, target) in enumerate(zip(sources, targets))
    ]
    fetch(0).start()
    for copy in copies:
        copy.start()

    @pl.loop(1, length)
    def _(tile):
        fetch(tile).start()

    make_plan(members, lengths_ref, hands_ref, plan_ref, choice_ref)
    for copy in copies:
        copy.wait()
    own, reply = tuple(targets[:2]), tuple(targets[2:])
    size_ref[QUERIES] = jnp.zeros((8, HEAD_WIDTH), jnp.float32)
    size_ref[KEYS] = largest_key_square([own, reply])
    size_ref[SCORES] = jnp.zeros((8, HEAD_WIDTH), jnp.float32)

    @pl.loop(0, length)
    def _(tile):
        fetch(tile).wait()
        largest = [size_ref[QUERIES]]

        def see(rows, scores):
            largest[0] = jnp.maximum(largest[0], largest_square(rows))

        attend_part(tile, held_ref, [own], reply, None, (mix_ref, total_ref), see)
        size_ref[QUERIES] = largest[0]


def next_body(pieces, lengths_ref, query_ref, *refs):
    blocks = list(zip(refs[: 2 * pieces : 2], refs[1 : 2 * pieces : 2]))
    state, target = refs[2 * pieces : 2 * pieces + 3], refs[2 * pieces + 3 :]
    size_ref = target[2]
    size_ref[...] = state[2][...]

    @pl.loop(0, lengths_ref[0, lax.axis_index("sample")])
    def _(tile):
        largest = [size_ref[SCORES]]

        def see(rows, scores):
            for block in scores:
                size = jnp.max(jnp.abs(block).reshape(-1, 8, block.shape[1]), axis=0)
                if block.shape[1] % HEAD_WIDTH:
                    size = jnp.max(size, axis=1, keepdims=True)
                width = min(size.shape[1], HEAD_WIDTH)
                for start in range(0, size.shape[1], width):
                    largest[0] = jnp.maximum(largest[0], size[:, start : start + width])

        attend_part(tile, query_ref, blocks, None, state, target, see)
        size_ref[SCORES] = largest[0]


def attend_part(tile, query_ref, blocks, reply, state, target, see=None):
    rows = rows_of(tile)
    mix_ref, total_ref = target[:2]
    lanes = lax.broadcasted_iota(jnp.int32, (TILE_TOKENS, HEAD_WIDTH), 1)
    totals = [jnp.zeros((TILE_TOKENS, HEAD_WIDTH), jnp.float32)]

    def done(index, where, mix, total):
        mix_ref[rows, where] = mix if state is None else mix + state[0][rows, where]
        totals[0] = jnp.where(lanes == index, total, totals[0])

    attend_tile(
        tile, query_ref.at[rows], blocks, reply, False, done, see, 2 if reply else QUERY_PER_KEY
    )
    total_ref[rows] = totals[0] if state is None else totals[0] + state[1][rows]


def finish_tile(tile, query_ref, blocks, mix_ref, total_ref, held_ref):
    rows = rows_of(tile)

    def done(index, where, mix, total):
        total = total + total_ref[rows, index : index + 1]
        held_ref[rows, where] = ((mix + mix_ref[rows, where]) * (1.0 / total)).astype(jnp.bfloat16)

    attend_tile(tile, query_ref.at[rows], blocks, None, False, done)


def last_body(pieces, others, plan_ref, query_ref, *refs):
    refs = list(refs)
    blocks = [(refs.pop(0), refs.pop(0)) for _ in range(pieces)]
    mix_ref, total_ref, size_ref = (refs.pop(0) for _ in range(3))
    far_refs = [refs.pop(0) for _ in range(2 * others)]
    size_out_ref, held_ref = refs.pop(0), refs.pop(0)
    send_refs = [refs.pop(0) for _ in range(PERMUTES)]
    near_refs = refs
    kept, live = plan_ref[KEPT], plan_ref[LIVE]
    keys = jnp.maximum(size_ref[KEYS], largest_key_square(blocks))
    squares = jnp.max(size_ref[QUERIES], axis=0, keepdims=True) * jnp.max(keys, axis=0, keepdims=True)
    size = jnp.maximum(jnp.sqrt(squares), jnp.max(size_ref[SCORES], axis=0, keepdims=True))
    size_out_ref[...] = jnp.broadcast_to(size, size_out_ref.shape)

    @pl.loop(kept, live)
    def _(tile):
        finish_tile(tile, query_ref, blocks, mix_ref, total_ref, held_ref)

    @pl.when(jnp.max(size) * SCALE > SAFE)
    def _():
        for source, target in zip(far_refs, near_refs):
            pltpu.sync_copy(source, target)
        pairs = list(zip(near_refs[::2], near_refs[1::2]))

        @pl.loop(0, live)
        def _(tile):
            rows = rows_of(tile)

            def done(index, where, mix, total):
                held_ref[rows, where] = (mix * (1.0 / total)).astype(jnp.bfloat16)

            attend_tile(tile, query_ref.at[rows], blocks + pairs[:-1], pairs[-1], True, done, heads=2)

    for index, send_ref in enumerate(send_refs):
        tile = plan_ref[SEND + index]

        @pl.when(tile >= 0)
        def _():
            send_ref[...] = held_ref[rows_of(tile)]


def kept_body(pieces, plan_ref, query_ref, *refs):
    refs = list(refs)
    blocks = [(refs.pop(0), refs.pop(0)) for _ in range(pieces)]
    mix_ref, total_ref, size_ref, done_ref, output_ref, held_ref, zero_ref, tile_sems = refs
    tiles = output_ref.shape[0] // TILE_TOKENS
    kept = plan_ref[KEPT]
    waiting = jnp.where(jnp.max(size_ref[...]) * SCALE > SAFE, 0, kept)

    def put(tile, source):
        return pltpu.make_async_copy(source, output_ref.at[rows_of(tile)], tile_sems.at[tile])

    zero_ref[...] = jnp.zeros(zero_ref.shape, zero_ref.dtype)

    @pl.loop(kept, tiles)
    def _(tile):
        put(tile, zero_ref).start()

    @pl.loop(waiting, kept)
    def _(tile):
        put(tile, done_ref.at[rows_of(tile)]).start()

    @pl.loop(0, waiting)
    def _(tile):
        rows = rows_of(tile)

        @pl.loop(0, HEADS)
        def _(head):
            where = pl.ds(pl.multiple_of(head * HEAD_WIDTH, HEAD_WIDTH), HEAD_WIDTH)
            group = head // QUERY_PER_KEY
            columns = pl.ds(pl.multiple_of(group * HEAD_WIDTH, HEAD_WIDTH), HEAD_WIDTH)
            lanes = lax.broadcasted_iota(jnp.int32, (TILE_TOKENS, HEAD_WIDTH), 1)
            total = jnp.sum(jnp.where(lanes == head, total_ref[rows], 0.0), axis=1, keepdims=True)
            mix = mix_ref[rows, where]
            for key_ref, value_ref in blocks:
                weights = lax.dot_general(
                    query_ref[rows, where],
                    key_ref[:, columns],
                    TRANSPOSED,
                    preferred_element_type=jnp.float32,
                )
                weights = jnp.exp2(weights * SCALE).astype(jnp.bfloat16)
                value = value_ref[:, columns]
                value = jnp.concatenate([value, jnp.ones(value.shape, value.dtype)], axis=1)
                more = jnp.dot(weights, value, preferred_element_type=jnp.float32)
                mix, total = mix + more[:, :HEAD_WIDTH], total + more[:, HEAD_WIDTH:]
            held_ref[rows, where] = (mix * (1.0 / total)).astype(jnp.bfloat16)

        put(tile, held_ref.at[rows]).start()

    @pl.loop(0, tiles)
    def _(tile):
        put(tile, zero_ref).wait()


IN_SMEM = pl.BlockSpec(memory_space=pltpu.SMEM)
IN_VMEM = pl.BlockSpec(memory_space=pltpu.VMEM)
ANYWHERE = pl.BlockSpec(memory_space=pl.ANY)


def attend(body, operands, in_specs, out_specs, out_shape, scratch, rows, keys):
    return pl.pallas_call(
        body,
        in_specs=in_specs,
        out_specs=out_specs,
        out_shape=out_shape,
        scratch_shapes=scratch,
        cost_estimate=pl.CostEstimate(
            flops=4 * rows * keys * COLUMNS,
            bytes_accessed=8 * rows * COLUMNS,
            transcendentals=rows * keys * HEADS,
        ),
        compiler_params=pltpu.CompilerParams(vmem_limit_bytes=24 << 20),
    )(*operands)


def state_shapes(rows):
    return [
        pltpu.VMEM((rows, COLUMNS), jnp.float32),
        pltpu.VMEM((rows, HEAD_WIDTH), jnp.float32),
        pltpu.VMEM((24, HEAD_WIDTH), jnp.float32),
    ]


def attend_first(members, lengths, hands, queries, own, reply):
    rows, arrays = queries.shape[0], [*own, *reply]
    plan, choice, queries_here, *state = attend(
        functools.partial(first_body, members),
        [lengths, hands, queries, *arrays],
        [IN_SMEM] * 2 + [ANYWHERE] * 5,
        [IN_SMEM] * 2 + [IN_VMEM] * 4,
        [jax.ShapeDtypeStruct((PLAN,), jnp.int32), jax.ShapeDtypeStruct((1,), jnp.int32)]
        + [pltpu.VMEM(queries.shape, queries.dtype)]
        + state_shapes(rows),
        [pltpu.VMEM(array.shape, array.dtype) for array in arrays]
        + [pltpu.SemaphoreType.DMA((4,)), pltpu.SemaphoreType.DMA((rows // TILE_TOKENS,))],
        rows,
        own[0].shape[0] + reply[0].shape[0],
    )
    return plan, choice, queries_here, state


def attend_next(lengths, queries, blocks, state):
    rows, arrays = queries.shape[0], [array for block in blocks for array in block]
    return attend(
        functools.partial(next_body, len(blocks)),
        [lengths, queries, *arrays, *state],
        [IN_SMEM] + [IN_VMEM] * (1 + len(arrays) + 3),
        [IN_VMEM] * 3,
        state_shapes(rows),
        [],
        rows,
        sum(block[0].shape[0] for block in blocks),
    )


def attend_last(plan, queries, blocks, others, state):
    rows, arrays = queries.shape[0], [array for block in blocks for array in block]
    earlier = [array for block in others for array in block]
    shape = (TILE_TOKENS, COLUMNS)
    size, done, *sends = attend(
        functools.partial(last_body, len(blocks), len(others)),
        [plan, queries, *arrays, *state, *earlier],
        [IN_SMEM] + [IN_VMEM] * (1 + len(arrays) + 3) + [ANYWHERE] * len(earlier),
        [IN_VMEM] * (2 + PERMUTES),
        [pltpu.VMEM((8, HEAD_WIDTH), jnp.float32), pltpu.VMEM(queries.shape, jnp.bfloat16)]
        + [pltpu.VMEM(shape, jnp.bfloat16)] * PERMUTES,
        [pltpu.VMEM(array.shape, array.dtype) for array in earlier],
        rows,
        sum(block[0].shape[0] for block in blocks),
    )
    return size, done, sends


def attend_kept(plan, queries, blocks, state, size, done):
    rows, arrays = queries.shape[0], [array for block in blocks for array in block]
    operands = [plan, queries, *arrays, *state[:2], size, done]
    return attend(
        functools.partial(kept_body, len(blocks)),
        operands,
        [IN_SMEM] + [IN_VMEM] * (len(operands) - 1),
        ANYWHERE,
        pltpu.HBM(queries.shape, jnp.bfloat16),
        [
            pltpu.VMEM(queries.shape, jnp.bfloat16),
            pltpu.VMEM((TILE_TOKENS, COLUMNS), jnp.bfloat16),
            pltpu.SemaphoreType.DMA((rows // TILE_TOKENS,)),
        ],
        rows,
        sum(block[0].shape[0] for block in blocks),
    )


def assemble_body(permutes, plan_ref, *refs):
    arrived, output, semaphores = refs[:permutes], refs[-2], refs[-1]
    copies = []
    for number in range(permutes):
        slot = plan_ref[FILL + number]
        first = pl.multiple_of(jnp.maximum(slot, 0) * TILE_TOKENS, TILE_TOKENS)
        copy = pltpu.make_async_copy(
            arrived[number], output.at[pl.ds(first, TILE_TOKENS)], semaphores.at[number]
        )
        copies.append((slot >= 0, copy))
    for taken, copy in copies:
        pl.when(taken)(copy.start)
    for taken, copy in copies:
        pl.when(taken)(copy.wait)


def assemble(plan, arrived, output, unused):
    return pl.pallas_call(
        functools.partial(assemble_body, len(arrived)),
        in_specs=[IN_SMEM] + [IN_VMEM] * len(arrived) + [ANYWHERE] * (1 + len(unused)),
        out_specs=ANYWHERE,
        out_shape=pltpu.HBM(output.shape, output.dtype),
        scratch_shapes=[pltpu.SemaphoreType.DMA((max(len(arrived), 1),))],
        input_output_aliases={len(arrived) + 1: 0},
        compiler_params=pltpu.CompilerParams(vmem_limit_bytes=1 << 20),
    )(plan, *arrived, output, *unused)


def swap(value, distance):
    members = lax.axis_size("sample")
    return lax.ppermute(value, "sample", [(source, source ^ distance) for source in range(members)])


def gather(own):
    held = [own]
    distance = lax.axis_size("sample") // 2
    while distance:
        held += [tuple(swap(array, distance) for array in block) for block in held]
        distance //= 2
    return held


def run_bundle(bundle, *operands):
    plan, sends, *rest = lax.optimization_barrier(operands)
    quarter = lax.axis_size("sample") // 4
    arrived = []
    for permute, tile in zip(bundle, sends):
        pairs = [
            (source * quarter + low, target * quarter + low)
            for source, target in permute
            for low in range(quarter)
        ]
        arrived.append(lax.ppermute(tile, "sample", pairs))
    output = attend_kept(plan, *rest)
    return assemble(plan, arrived, output, sends[len(bundle) :])


def run_chain(*operands):
    plan, sends, *rest = lax.optimization_barrier(operands)
    output = assemble(plan, [], attend_kept(plan, *rest), sends)
    for section in range(SECTIONS):
        distance = lax.axis_size("sample") >> (section + 1)

        def trade(count, output, keeping, distance=distance):
            if count == 0:
                return output
            top_rows = lax.dynamic_slice_in_dim(
                output, keeping * TILE_TOKENS, count * TILE_TOKENS, 0
            )
            return lax.dynamic_update_slice_in_dim(
                output, swap(top_rows, distance), keeping * TILE_TOKENS, 0
            )

        output = lax.switch(
            plan[TRADED + section],
            [functools.partial(trade, count) for count in range(HAND + 1)],
            output,
            plan[KEEPING + section],
        )
    return output


def per_device(
    queries, prompt_keys, prompt_value_rows, reply_keys, response_values, lengths, hand_counts
):
    members = lax.axis_size("sample")
    held = gather((prompt_keys[0], prompt_value_rows[0]))
    queries, *own = (
        pltpu.with_memory_space_constraint(array[0], pltpu.HBM)
        for array in (queries, prompt_keys, prompt_value_rows, reply_keys, response_values)
    )
    own, reply = tuple(own[:2]), tuple(own[2:])
    lengths = pltpu.with_memory_space_constraint(lengths, pltpu.HBM)
    held[0] = own
    half = members // 2 + 1
    hands = pltpu.with_memory_space_constraint(jnp.swapaxes(hand_counts, 1, 2), pltpu.HBM)
    plan, choice, queries, state = attend_first(members, lengths, hands, queries, own, reply)
    state = attend_next(lengths, queries, held[1:half], state)
    size, done, sends = attend_last(plan, queries, held[half:], held[:half] + [reply], state)
    output = lax.switch(
        choice[0],
        [functools.partial(run_bundle, bundle) for bundle in BUNDLES] + [run_chain],
        plan,
        sends,
        queries,
        held[half:],
        state,
        size,
        done,
    )
    return output[None]


def solution(mesh):
    placed = (
        P("prompt", "sample", None),
        P("prompt", "sample", None),
        P("prompt", "sample", None),
        P("prompt", "sample", None),
        P("prompt", "sample", None),
        P("prompt", None),
        P("prompt", None, None),
    )
    return jax.shard_map(
        per_device,
        mesh=mesh,
        in_specs=placed,
        out_specs=P("prompt", "sample", None),
        check_vma=False,
    )
```

```python
import functools
import math

import jax
import jax.numpy as jnp
from jax import lax
from jax.experimental import pallas as pl
from jax.experimental.pallas import tpu as pltpu
from jax.sharding import PartitionSpec as P

KEY_VALUE_HEADS = 2
QUERY_PER_KEY = 7
HEAD_WIDTH = 128
TILE_TOKENS = 128
MOST_TILES = 4
SECTIONS = 2
HAND = 2
HEADS = KEY_VALUE_HEADS * QUERY_PER_KEY
COLUMNS = HEADS * HEAD_WIDTH
SCALE = math.log2(math.e) / math.sqrt(HEAD_WIDTH)
MASKED = -1e30
QUERIES, KEYS, SCORES = slice(0, 8), slice(8, 16), slice(16, 24)
SAFE = 100.0
TRANSPOSED = (((1,), (1,)), ((), ()))
def jobs(heads):
    return tuple(
        (group, head, min(head + heads, QUERY_PER_KEY))
        for group in range(KEY_VALUE_HEADS)
        for head in range(0, QUERY_PER_KEY, heads)
    )


FAR = ((0, 2), (2, 0), (1, 3), (3, 1))
NEAR = ((0, 1), (1, 0), (2, 3), (3, 2))
CROSS = ((0, 3), (3, 0), (1, 2), (2, 1))


def usual_bundles():
    trades = {
        (): ((), ((0, 1),), ((1, 0),), ((3, 0),)),
        ((1, 3),): ((), ((0, 1),), ((1, 0),)),
        ((3, 1),): ((), ((3, 0),)),
    }
    bundles = []
    for beside, others in trades.items():
        for more in others:
            far, onward = ((0, 2),) + beside, ((0, 3),)
            bundles.append((far, ((0, 2),)) + ((more,) if more else ()))
            if more == ((3, 0),):
                bundles.append((far, onward + more))
            else:
                bundles.append((far, onward) + ((more,) if more else ()))
    return sorted(bundles, key=lambda bundle: (len(bundle), sum(map(len, bundle))))


BUNDLES = (
    *usual_bundles(),
    (((0, 2), (1, 3)), ((0, 2), (1, 3))),
    (((0, 2), (3, 1)), ((0, 2), (3, 1)), ((0, 3), (3, 0))),
    (((0, 2),), ((0, 2),), ((1, 0), (3, 2)), ((1, 2),)),
    (FAR, FAR, CROSS, NEAR),
)
PERMUTES = max(len(bundle) for bundle in BUNDLES)
SEND, FILL, KEPT = 0, PERMUTES, 2 * PERMUTES
LIVE = KEPT + 1
TRADED = LIVE + 1
KEEPING = TRADED + SECTIONS
PLAN = KEEPING + SECTIONS


def bundle_entries(bundle):
    entries, capacity = [], {}
    for permute in bundle:
        (distance,) = {source ^ target for source, target in permute}
        turn = sum(1 for other, _ in entries if other == distance)
        entries.append((distance, turn))
        for source, _ in permute:
            assert capacity.get((source, distance), 0) == turn
            capacity[source, distance] = turn + 1
    return entries, capacity


def make_plan(members, lengths_ref, hands_ref, plan_ref, choice_ref):
    me = lax.axis_index("sample")
    far, near = members // 2, members // 4

    def counts(device):
        partner = device ^ far
        first = hands_ref[0, 0, device]
        through = jnp.minimum(hands_ref[0, 1, partner], first)
        second = jnp.maximum(hands_ref[0, 1, device] - hands_ref[0, 0, partner], 0)
        return {1: second, 2: first - through, 3: through}

    needs = {}
    for device in range(members):
        for distance, count in counts(device).items():
            key = (device // near, distance)
            needs[key] = jnp.maximum(needs[key], count) if key in needs else count
    choice = jnp.int32(len(BUNDLES))
    for number in reversed(range(len(BUNDLES))):
        _, capacity = bundle_entries(BUNDLES[number])
        lacking = jnp.int32(0)
        for key, count in needs.items():
            lacking = lacking + jnp.maximum(count - capacity.get(key, 0), 0)
        choice = jnp.where(lacking == 0, number, choice)
    choice_ref[0] = choice

    mine = counts(me)
    length = lengths_ref[0, me]
    kept = length - mine[1] - mine[2] - mine[3]
    arriving = {2: counts(me ^ far)[2], 1: counts(me ^ near)[1], 3: counts(me ^ far ^ near)[3]}
    first_tile, first_slot = {}, {}
    tile = slot = kept
    for distance in (1, 2, 3):
        first_tile[distance] = tile
        tile = tile + mine[distance]
    for distance in (2, 1, 3):
        first_slot[distance] = slot
        slot = slot + arriving[distance]
    for index in range(PERMUTES):
        send = fill = jnp.int32(-1)
        for number, bundle in enumerate(BUNDLES):
            entries, _ = bundle_entries(bundle)
            if index < len(entries):
                distance, turn = entries[index]
                here = choice == number
                leaves = jnp.where(turn < mine[distance], first_tile[distance] + turn, -1)
                enters = jnp.where(turn < arriving[distance], first_slot[distance] + turn, -1)
                send = jnp.where(here, leaves, send)
                fill = jnp.where(here, enters, fill)
        plan_ref[SEND + index] = send
        plan_ref[FILL + index] = fill
    plan_ref[KEPT] = jnp.where(choice == len(BUNDLES), length, kept)
    plan_ref[LIVE] = length
    load = length
    for section in range(SECTIONS):
        giving = hands_ref[0, section, me]
        getting = hands_ref[0, section, me ^ (members >> (section + 1))]
        plan_ref[TRADED + section] = jnp.maximum(giving, getting)
        plan_ref[KEEPING + section] = load - giving
        load = load - giving + getting


def head_columns(group, head):
    first = (group * QUERY_PER_KEY + head) * HEAD_WIDTH
    return slice(first, first + HEAD_WIDTH)


def attend_tile(tile, query_ref, blocks, reply, with_max, done, see=None, heads=QUERY_PER_KEY):
    pairs = blocks + ([reply] if reply is not None else [])

    def score(job):
        group, first, last = job
        columns = slice(group * HEAD_WIDTH, (group + 1) * HEAD_WIDTH)
        rows = jnp.concatenate(
            [query_ref[:, head_columns(group, head)] for head in range(first, last)], axis=0
        )
        scores = [
            lax.dot_general(
                rows, keys[:, columns], TRANSPOSED, preferred_element_type=jnp.float32
            )
            for keys, _ in pairs
        ]
        if see is not None:
            see(rows, scores)
        if reply is not None:
            shape = (TILE_TOKENS, scores[-1].shape[1])
            ahead = lax.broadcasted_iota(jnp.int32, shape, 1) - lax.broadcasted_iota(
                jnp.int32, shape, 0
            )
            bias = jnp.where(ahead <= tile * TILE_TOKENS, 0.0, MASKED)
            scores[-1] = scores[-1] + jnp.concatenate([bias] * (last - first), axis=0)
        return scores

    def finish(job, scores):
        group, first, last = job
        columns = slice(group * HEAD_WIDTH, (group + 1) * HEAD_WIDTH)
        if with_max:
            top = functools.reduce(
                jnp.maximum, [jnp.max(block, axis=1, keepdims=True) for block in scores]
            )
            scores = [block - top for block in scores]
        mix = 0.0
        for block, (_, value) in zip(scores, pairs):
            weights = jnp.exp2(block * SCALE).astype(jnp.bfloat16)
            value = jnp.concatenate(
                [value[:, columns], jnp.ones((value.shape[0], HEAD_WIDTH), jnp.bfloat16)], axis=1
            )
            mix = mix + jnp.dot(weights, value, preferred_element_type=jnp.float32)
        for head in range(first, last):
            part = slice((head - first) * TILE_TOKENS, (head - first + 1) * TILE_TOKENS)
            index = group * QUERY_PER_KEY + head
            done(index, head_columns(group, head), mix[part, :HEAD_WIDTH], mix[part, HEAD_WIDTH:])

    turns = jobs(heads)
    ahead = score(turns[0])
    for number, job in enumerate(turns):
        scores = ahead
        if number + 1 < len(turns):
            ahead = score(turns[number + 1])
        finish(job, scores)


def rows_of(tile):
    return pl.ds(pl.multiple_of(tile * TILE_TOKENS, TILE_TOKENS), TILE_TOKENS)


def largest_square(rows):
    rows = rows.astype(jnp.float32)
    squares = jnp.sum(rows * rows, axis=1, keepdims=True)
    squares = jnp.max(squares.reshape(-1, 8, 1), axis=0)
    return jnp.broadcast_to(squares, (8, HEAD_WIDTH))


def largest_key_square(blocks):
    return functools.reduce(
        jnp.maximum,
        [
            largest_square(keys[:, group * HEAD_WIDTH : (group + 1) * HEAD_WIDTH])
            for keys, _ in blocks
            for group in range(KEY_VALUE_HEADS)
        ],
    )


def first_body(members, lengths_ref, hands_ref, query_ref, *refs):
    sources, refs = refs[:4], refs[4:]
    plan_ref, choice_ref, held_ref, mix_ref, total_ref, size_ref, *targets = refs
    targets, (block_sems, tile_sems) = targets[:4], targets[4:]
    length = lengths_ref[0, lax.axis_index("sample")]

    def fetch(tile):
        rows = rows_of(tile)
        return pltpu.make_async_copy(query_ref.at[rows], held_ref.at[rows], tile_sems.at[tile])

    copies = [
        pltpu.make_async_copy(source, target, block_sems.at[number])
        for number, (source, target) in enumerate(zip(sources, targets))
    ]
    fetch(0).start()
    for copy in copies:
        copy.start()

    @pl.loop(1, length)
    def _(tile):
        fetch(tile).start()

    make_plan(members, lengths_ref, hands_ref, plan_ref, choice_ref)
    for copy in copies:
        copy.wait()
    own, reply = tuple(targets[:2]), tuple(targets[2:])
    size_ref[QUERIES] = jnp.zeros((8, HEAD_WIDTH), jnp.float32)
    size_ref[KEYS] = largest_key_square([own, reply])
    size_ref[SCORES] = jnp.zeros((8, HEAD_WIDTH), jnp.float32)

    @pl.loop(0, length)
    def _(tile):
        fetch(tile).wait()
        largest = [size_ref[QUERIES]]

        def see(rows, scores):
            largest[0] = jnp.maximum(largest[0], largest_square(rows))

        attend_part(tile, held_ref, [own], reply, None, (mix_ref, total_ref), see)
        size_ref[QUERIES] = largest[0]


def next_body(pieces, lengths_ref, query_ref, *refs):
    blocks = list(zip(refs[: 2 * pieces : 2], refs[1 : 2 * pieces : 2]))
    state, target = refs[2 * pieces : 2 * pieces + 3], refs[2 * pieces + 3 :]
    size_ref = target[2]
    size_ref[...] = state[2][...]

    @pl.loop(0, lengths_ref[0, lax.axis_index("sample")])
    def _(tile):
        largest = [size_ref[SCORES]]

        def see(rows, scores):
            for block in scores:
                size = jnp.max(jnp.abs(block).reshape(-1, 8, block.shape[1]), axis=0)
                if block.shape[1] % HEAD_WIDTH:
                    size = jnp.max(size, axis=1, keepdims=True)
                width = min(size.shape[1], HEAD_WIDTH)
                for start in range(0, size.shape[1], width):
                    largest[0] = jnp.maximum(largest[0], size[:, start : start + width])

        attend_part(tile, query_ref, blocks, None, state, target, see)
        size_ref[SCORES] = largest[0]


def attend_part(tile, query_ref, blocks, reply, state, target, see=None):
    rows = rows_of(tile)
    mix_ref, total_ref = target[:2]
    lanes = lax.broadcasted_iota(jnp.int32, (TILE_TOKENS, HEAD_WIDTH), 1)
    totals = [jnp.zeros((TILE_TOKENS, HEAD_WIDTH), jnp.float32)]

    def done(index, where, mix, total):
        mix_ref[rows, where] = mix if state is None else mix + state[0][rows, where]
        totals[0] = jnp.where(lanes == index, total, totals[0])

    attend_tile(
        tile, query_ref.at[rows], blocks, reply, False, done, see, 2 if reply else QUERY_PER_KEY
    )
    total_ref[rows] = totals[0] if state is None else totals[0] + state[1][rows]


def finish_tile(tile, query_ref, blocks, mix_ref, total_ref, held_ref):
    rows = rows_of(tile)

    def done(index, where, mix, total):
        total = total + total_ref[rows, index : index + 1]
        held_ref[rows, where] = ((mix + mix_ref[rows, where]) * (1.0 / total)).astype(jnp.bfloat16)

    attend_tile(tile, query_ref.at[rows], blocks, None, False, done)


def last_body(pieces, others, plan_ref, query_ref, *refs):
    refs = list(refs)
    blocks = [(refs.pop(0), refs.pop(0)) for _ in range(pieces)]
    mix_ref, total_ref, size_ref = (refs.pop(0) for _ in range(3))
    far_refs = [refs.pop(0) for _ in range(2 * others)]
    size_out_ref, held_ref = refs.pop(0), refs.pop(0)
    send_refs = [refs.pop(0) for _ in range(PERMUTES)]
    near_refs = refs
    kept, live = plan_ref[KEPT], plan_ref[LIVE]
    keys = jnp.maximum(size_ref[KEYS], largest_key_square(blocks))
    squares = jnp.max(size_ref[QUERIES], axis=0, keepdims=True) * jnp.max(keys, axis=0, keepdims=True)
    size = jnp.maximum(jnp.sqrt(squares), jnp.max(size_ref[SCORES], axis=0, keepdims=True))
    size_out_ref[...] = jnp.broadcast_to(size, size_out_ref.shape)

    @pl.loop(kept, live)
    def _(tile):
        finish_tile(tile, query_ref, blocks, mix_ref, total_ref, held_ref)

    @pl.when(jnp.max(size) * SCALE > SAFE)
    def _():
        for source, target in zip(far_refs, near_refs):
            pltpu.sync_copy(source, target)
        pairs = list(zip(near_refs[::2], near_refs[1::2]))

        @pl.loop(0, live)
        def _(tile):
            rows = rows_of(tile)

            def done(index, where, mix, total):
                held_ref[rows, where] = (mix * (1.0 / total)).astype(jnp.bfloat16)

            attend_tile(tile, query_ref.at[rows], blocks + pairs[:-1], pairs[-1], True, done, heads=2)

    for index, send_ref in enumerate(send_refs):
        tile = plan_ref[SEND + index]

        @pl.when(tile >= 0)
        def _():
            send_ref[...] = held_ref[rows_of(tile)]


def kept_body(pieces, plan_ref, query_ref, *refs):
    refs = list(refs)
    blocks = [(refs.pop(0), refs.pop(0)) for _ in range(pieces)]
    mix_ref, total_ref, size_ref, done_ref, output_ref, held_ref, zero_ref, tile_sems = refs
    tiles = output_ref.shape[0] // TILE_TOKENS
    kept = plan_ref[KEPT]
    waiting = jnp.where(jnp.max(size_ref[...]) * SCALE > SAFE, 0, kept)

    def put(tile, source):
        return pltpu.make_async_copy(source, output_ref.at[rows_of(tile)], tile_sems.at[tile])

    zero_ref[...] = jnp.zeros(zero_ref.shape, zero_ref.dtype)

    @pl.loop(kept, tiles)
    def _(tile):
        put(tile, zero_ref).start()

    @pl.loop(waiting, kept)
    def _(tile):
        put(tile, done_ref.at[rows_of(tile)]).start()

    @pl.loop(0, waiting)
    def _(tile):
        rows = rows_of(tile)

        @pl.loop(0, HEADS)
        def _(head):
            where = pl.ds(pl.multiple_of(head * HEAD_WIDTH, HEAD_WIDTH), HEAD_WIDTH)
            group = head // QUERY_PER_KEY
            columns = pl.ds(pl.multiple_of(group * HEAD_WIDTH, HEAD_WIDTH), HEAD_WIDTH)
            lanes = lax.broadcasted_iota(jnp.int32, (TILE_TOKENS, HEAD_WIDTH), 1)
            total = jnp.sum(jnp.where(lanes == head, total_ref[rows], 0.0), axis=1, keepdims=True)
            mix = mix_ref[rows, where]
            for key_ref, value_ref in blocks:
                weights = lax.dot_general(
                    query_ref[rows, where],
                    key_ref[:, columns],
                    TRANSPOSED,
                    preferred_element_type=jnp.float32,
                )
                weights = jnp.exp2(weights * SCALE).astype(jnp.bfloat16)
                value = value_ref[:, columns]
                value = jnp.concatenate([value, jnp.ones(value.shape, value.dtype)], axis=1)
                more = jnp.dot(weights, value, preferred_element_type=jnp.float32)
                mix, total = mix + more[:, :HEAD_WIDTH], total + more[:, HEAD_WIDTH:]
            held_ref[rows, where] = (mix * (1.0 / total)).astype(jnp.bfloat16)

        put(tile, held_ref.at[rows]).start()

    @pl.loop(0, tiles)
    def _(tile):
        put(tile, zero_ref).wait()


IN_SMEM = pl.BlockSpec(memory_space=pltpu.SMEM)
IN_VMEM = pl.BlockSpec(memory_space=pltpu.VMEM)
ANYWHERE = pl.BlockSpec(memory_space=pl.ANY)


def attend(body, operands, in_specs, out_specs, out_shape, scratch, rows, keys):
    return pl.pallas_call(
        body,
        in_specs=in_specs,
        out_specs=out_specs,
        out_shape=out_shape,
        scratch_shapes=scratch,
        cost_estimate=pl.CostEstimate(
            flops=4 * rows * keys * COLUMNS,
            bytes_accessed=8 * rows * COLUMNS,
            transcendentals=rows * keys * HEADS,
        ),
        compiler_params=pltpu.CompilerParams(vmem_limit_bytes=24 << 20),
    )(*operands)


def state_shapes(rows):
    return [
        pltpu.VMEM((rows, COLUMNS), jnp.float32),
        pltpu.VMEM((rows, HEAD_WIDTH), jnp.float32),
        pltpu.VMEM((24, HEAD_WIDTH), jnp.float32),
    ]


def attend_first(members, lengths, hands, queries, own, reply):
    rows, arrays = queries.shape[0], [*own, *reply]
    plan, choice, queries_here, *state = attend(
        functools.partial(first_body, members),
        [lengths, hands, queries, *arrays],
        [IN_SMEM] * 2 + [ANYWHERE] * 5,
        [IN_SMEM] * 2 + [IN_VMEM] * 4,
        [jax.ShapeDtypeStruct((PLAN,), jnp.int32), jax.ShapeDtypeStruct((1,), jnp.int32)]
        + [pltpu.VMEM(queries.shape, queries.dtype)]
        + state_shapes(rows),
        [pltpu.VMEM(array.shape, array.dtype) for array in arrays]
        + [pltpu.SemaphoreType.DMA((4,)), pltpu.SemaphoreType.DMA((rows // TILE_TOKENS,))],
        rows,
        own[0].shape[0] + reply[0].shape[0],
    )
    return plan, choice, queries_here, state


def attend_next(lengths, queries, blocks, state):
    rows, arrays = queries.shape[0], [array for block in blocks for array in block]
    return attend(
        functools.partial(next_body, len(blocks)),
        [lengths, queries, *arrays, *state],
        [IN_SMEM] + [IN_VMEM] * (1 + len(arrays) + 3),
        [IN_VMEM] * 3,
        state_shapes(rows),
        [],
        rows,
        sum(block[0].shape[0] for block in blocks),
    )


def attend_last(plan, queries, blocks, others, state):
    rows, arrays = queries.shape[0], [array for block in blocks for array in block]
    earlier = [array for block in others for array in block]
    shape = (TILE_TOKENS, COLUMNS)
    size, done, *sends = attend(
        functools.partial(last_body, len(blocks), len(others)),
        [plan, queries, *arrays, *state, *earlier],
        [IN_SMEM] + [IN_VMEM] * (1 + len(arrays) + 3) + [ANYWHERE] * len(earlier),
        [IN_VMEM] * (2 + PERMUTES),
        [pltpu.VMEM((8, HEAD_WIDTH), jnp.float32), pltpu.VMEM(queries.shape, jnp.bfloat16)]
        + [pltpu.VMEM(shape, jnp.bfloat16)] * PERMUTES,
        [pltpu.VMEM(array.shape, array.dtype) for array in earlier],
        rows,
        sum(block[0].shape[0] for block in blocks),
    )
    return size, done, sends


def attend_kept(plan, queries, blocks, state, size, done):
    rows, arrays = queries.shape[0], [array for block in blocks for array in block]
    operands = [plan, queries, *arrays, *state[:2], size, done]
    return attend(
        functools.partial(kept_body, len(blocks)),
        operands,
        [IN_SMEM] + [IN_VMEM] * (len(operands) - 1),
        ANYWHERE,
        pltpu.HBM(queries.shape, jnp.bfloat16),
        [
            pltpu.VMEM(queries.shape, jnp.bfloat16),
            pltpu.VMEM((TILE_TOKENS, COLUMNS), jnp.bfloat16),
            pltpu.SemaphoreType.DMA((rows // TILE_TOKENS,)),
        ],
        rows,
        sum(block[0].shape[0] for block in blocks),
    )


def assemble_body(permutes, plan_ref, *refs):
    arrived, output, semaphores = refs[:permutes], refs[-2], refs[-1]
    copies = []
    for number in range(permutes):
        slot = plan_ref[FILL + number]
        first = pl.multiple_of(jnp.maximum(slot, 0) * TILE_TOKENS, TILE_TOKENS)
        copy = pltpu.make_async_copy(
            arrived[number], output.at[pl.ds(first, TILE_TOKENS)], semaphores.at[number]
        )
        copies.append((slot >= 0, copy))
    for taken, copy in copies:
        pl.when(taken)(copy.start)
    for taken, copy in copies:
        pl.when(taken)(copy.wait)


def assemble(plan, arrived, output, unused):
    return pl.pallas_call(
        functools.partial(assemble_body, len(arrived)),
        in_specs=[IN_SMEM] + [IN_VMEM] * len(arrived) + [ANYWHERE] * (1 + len(unused)),
        out_specs=ANYWHERE,
        out_shape=pltpu.HBM(output.shape, output.dtype),
        scratch_shapes=[pltpu.SemaphoreType.DMA((max(len(arrived), 1),))],
        input_output_aliases={len(arrived) + 1: 0},
        compiler_params=pltpu.CompilerParams(vmem_limit_bytes=1 << 20),
    )(plan, *arrived, output, *unused)


def swap(value, distance):
    members = lax.axis_size("sample")
    return lax.ppermute(value, "sample", [(source, source ^ distance) for source in range(members)])


def gather(own):
    held = [own]
    distance = lax.axis_size("sample") // 2
    while distance:
        held += [tuple(swap(array, distance) for array in block) for block in held]
        distance //= 2
    return held


def run_bundle(bundle, *operands):
    plan, sends, *rest = lax.optimization_barrier(operands)
    quarter = lax.axis_size("sample") // 4
    arrived = []
    for permute, tile in zip(bundle, sends):
        pairs = [
            (source * quarter + low, target * quarter + low)
            for source, target in permute
            for low in range(quarter)
        ]
        arrived.append(lax.ppermute(tile, "sample", pairs))
    output = attend_kept(plan, *rest)
    return assemble(plan, arrived, output, sends[len(bundle) :])


def run_chain(*operands):
    plan, sends, *rest = lax.optimization_barrier(operands)
    output = assemble(plan, [], attend_kept(plan, *rest), sends)
    for section in range(SECTIONS):
        distance = lax.axis_size("sample") >> (section + 1)

        def trade(count, output, keeping, distance=distance):
            if count == 0:
                return output
            top_rows = lax.dynamic_slice_in_dim(
                output, keeping * TILE_TOKENS, count * TILE_TOKENS, 0
            )
            return lax.dynamic_update_slice_in_dim(
                output, swap(top_rows, distance), keeping * TILE_TOKENS, 0
            )

        output = lax.switch(
            plan[TRADED + section],
            [functools.partial(trade, count) for count in range(HAND + 1)],
            output,
            plan[KEEPING + section],
        )
    return output


def per_device(
    queries, prompt_keys, prompt_value_rows, reply_keys, response_values, lengths, hand_counts
):
    members = lax.axis_size("sample")
    held = gather((prompt_keys[0], prompt_value_rows[0]))
    queries, *own = (
        pltpu.with_memory_space_constraint(array[0], pltpu.HBM)
        for array in (queries, prompt_keys, prompt_value_rows, reply_keys, response_values)
    )
    own, reply = tuple(own[:2]), tuple(own[2:])
    lengths = pltpu.with_memory_space_constraint(lengths, pltpu.HBM)
    held[0] = own
    half = members // 2 + 1
    hands = pltpu.with_memory_space_constraint(jnp.swapaxes(hand_counts, 1, 2), pltpu.HBM)
    plan, choice, queries, state = attend_first(members, lengths, hands, queries, own, reply)
    state = attend_next(lengths, queries, held[1:half], state)
    size, done, sends = attend_last(plan, queries, held[half:], held[:half] + [reply], state)
    output = lax.switch(
        choice[0],
        [functools.partial(run_bundle, bundle) for bundle in BUNDLES] + [run_chain],
        plan,
        sends,
        queries,
        held[half:],
        state,
        size,
        done,
    )
    return output[None]


def solution(mesh):
    placed = (
        P("prompt", "sample", None),
        P("prompt", "sample", None),
        P("prompt", "sample", None),
        P("prompt", "sample", None),
        P("prompt", "sample", None),
        P("prompt", None),
        P("prompt", None, None),
    )
    return jax.shard_map(
        per_device,
        mesh=mesh,
        in_specs=placed,
        out_specs=P("prompt", "sample", None),
        check_vma=False,
    )
```
